32 devices in a mesh: ctx: 16 (over z, x, core), kv: 2 (over y).
Axes of the slice: x: 2, y: 2, z: 4, core: 2. Of those that a mesh axis runs over, the one named last changes fastest.
Arguments:
- queries: bfloat16 [3072, 5120], P('ctx', 'kv'), may hold values from -16 to 16
- keys: bfloat16 [3072, 1024], P('ctx', 'kv'), may hold values from -8 to 8
- values: bfloat16 [3072, 1024], P('ctx', 'kv'), may hold values from -6 to 6
- w_out: bfloat16 [5120, 5120], P('kv', 'ctx'), may hold values from -0.078125 to 0.078125
- grad_y: bfloat16 [3072, 5120], P('ctx', 'kv'), may hold values from -6 to 6
- resp_blocks: int32 [4], replicated, may hold values from 1 to 6, 12 in all
Outputs:
- y_out: bfloat16 [3072, 5120], P('ctx', 'kv')
- grad_q: bfloat16 [3072, 5120], P('ctx', 'kv')
- grad_k: bfloat16 [3072, 1024], P('ctx', 'kv')
- grad_v: bfloat16 [3072, 1024], P('ctx', 'kv')
The draws below stay inside these ranges and needn't reach their ends.
Inputs may be any that keep to these rules, and one draw needn't show every extreme that they name: resp_blocks sums to 12; the longest response has exactly 6 blocks.
All inputs are finite; a program needn't handle non-finite values.
Results may differ from the reference program's by a relative error of at most 0.035.
Values may be sent and summed in bfloat16 or wider, within the bound.
A program may use at most 128 MiB of HBM per device.

```python
import math
import jax
import jax.numpy as jnp
import numpy as np
from jax import lax

D = 5120
H = 40
KVH = 8
HD = 128
BLK = 128
NRESP = 4
TOK_DEV = 192
TOKENS = 3072
PROMPT = 1536
RESP_BLOCKS = 12
MOST_BLOCKS = 6
N_KV = 2


def paired_draw(key):
    key_vals = jnp.clip(jax.random.normal(jax.random.fold_in(key, 11), (TOKENS, KVH * HD), jnp.float32), -4.5, 4.5)
    query_vals = jnp.clip(jax.random.normal(jax.random.fold_in(key, 12), (TOKENS, H * HD), jnp.float32), -4.5, 4.5)
    return (query_vals, key_vals)


def draw_queries(key, part):
    return paired_draw(key)[0].astype(jnp.bfloat16)


def draw_keys(key, part):
    return paired_draw(key)[1].astype(jnp.bfloat16)


def level_of(rng, dims, shards, smallest, largest):
    level = 1.0
    for position, shards_of in shards:
        steps = jax.random.uniform(jax.random.fold_in(jax.random.fold_in(rng, 6), position), (shards_of,), jnp.float32, smallest / len(shards), largest / len(shards))
        level = level * jnp.repeat(jnp.exp(steps), dims[position] // shards_of).reshape((-1,) + (1,) * (len(dims) - 1 - position))
    return level


def length_profile(number_of, total, bound, skew):
    loads = [(1 << 20) // math.isqrt(rank ** skew) + 1 for rank in range(2, number_of + 1)]
    rest, holding = total - bound - (number_of - 1), [1] * (number_of - 1)
    while rest > 0:
        candidates = [i for i in range(number_of - 1) if holding[i] < bound]
        whole, budget = sum([loads[i] for i in candidates]), rest
        for i in candidates:
            more = min(bound - holding[i], max(1, budget * loads[i] // whole), rest)
            holding[i] = holding[i] + more
            rest = rest - more
    return np.array([bound] + holding)


def uneven_parts(stream_key, count, total, reach, skew):
    if count == 2:
        one = jax.random.randint(stream_key, (), max(1, total - reach), min(reach, total - 1) + 1)
        return jnp.stack([one, total - one])
    lengths = jnp.asarray(length_profile(count, total, reach, skew), jnp.int32)
    twos = (count - 1) // 2
    source_of, taker = lengths[1:1 + 2 * twos:2], lengths[2:2 + 2 * twos:2]
    slack = jnp.minimum(source_of - 1, reach - taker)
    passed = jax.random.randint(jax.random.fold_in(stream_key, 1), (twos,), 0, 1 << 20) % (slack + 1)
    lengths = lengths.at[1:1 + 2 * twos:2].set(source_of - passed).at[2:2 + 2 * twos:2].set(taker + passed)
    return lengths[jax.random.permutation(jax.random.fold_in(stream_key, 2), count)]


def normal_values(own_key, dims, spread, reach, cuts=(), kind=jnp.bfloat16):
    array = spread * jax.random.normal(own_key, dims, jnp.float32)
    if cuts:
        array = array * level_of(own_key, dims, cuts, -0.22, 0.18)
    return jnp.clip(array, -reach, reach).astype(kind)


def setup_inputs(seed: int = 0) -> dict:
    seeds = jax.random.split(jax.random.key(seed), 7)
    queries = draw_queries(jax.random.fold_in(seeds[6], 71), 0)
    keys = draw_keys(jax.random.fold_in(seeds[6], 71), 0)
    values = normal_values(seeds[2], (TOKENS, KVH * HD), 1.0, 6.0, ((0, 16), (1, 2)))
    w_out = normal_values(seeds[3], (H * HD, D), (H * HD) ** -0.5, 0.078125, ((0, 2), (1, 16)))
    grad_y = normal_values(seeds[4], (TOKENS, D), 1.0, 6.0, ((0, 16), (1, 2)))
    resp_blocks = uneven_parts(seeds[5], NRESP, RESP_BLOCKS, MOST_BLOCKS, 1).astype(jnp.int32)
    return dict(queries=queries, keys=keys, values=values, w_out=w_out, grad_y=grad_y, resp_blocks=resp_blocks)


NEG = -1e+30

def segment_ids(positions, resp_blocks, prompt_len):
    resp_ends = jnp.cumsum(resp_blocks).astype(jnp.int32) * BLK
    offsets = positions - prompt_len
    later = lax.optimization_barrier(jnp.sum((offsets[:, None] >= resp_ends[None, :NRESP - 1]).astype(jnp.int32), axis=1))
    return jnp.where(positions < prompt_len, 0, 1 + later).astype(jnp.int32)

def visible_pairs(query_pos, query_seg, key_pos, key_seg):
    causal = key_pos[None, :] <= query_pos[:, None]
    same = (key_seg[None, :] == 0) | (key_seg[None, :] == query_seg[:, None])
    return causal & same

def rounded(values_in):
    return lax.optimization_barrier(values_in.astype(jnp.bfloat16)).astype(jnp.float32)

def reference(queries, keys, values, w_out, grad_y, resp_blocks):
    group_size = H // KVH
    score_scale = 1.0 / math.sqrt(HD)
    qblock = TOK_DEV
    block_total = TOKENS // qblock
    positions = jnp.arange(TOKENS, dtype=jnp.int32)
    segments = segment_ids(positions, resp_blocks, PROMPT)
    grad_attn = jnp.dot(grad_y, w_out.T, preferred_element_type=jnp.float32).astype(jnp.bfloat16)
    q_heads = queries.reshape(TOKENS, KVH, group_size, HD).transpose(1, 0, 2, 3)
    d_heads = grad_attn.reshape(TOKENS, KVH, group_size, HD).transpose(1, 0, 2, 3)
    k_heads = keys.reshape(TOKENS, KVH, HD).transpose(1, 0, 2)
    v_heads = values.reshape(TOKENS, KVH, HD).transpose(1, 0, 2)

    def one_head(operands):
        q_one, k_one, v_one, d_one = operands
        k_full = k_one.astype(jnp.float32)
        v_full = v_one.astype(jnp.float32)

        def one_block(grads, block_index):
            first = (block_index * qblock).astype(jnp.int32)
            q_rows = lax.dynamic_slice_in_dim(q_one, first, qblock, 0).astype(jnp.float32)
            d_rows = lax.dynamic_slice_in_dim(d_one, first, qblock, 0).astype(jnp.float32)
            query_pos = first + jnp.arange(qblock, dtype=jnp.int32)
            query_seg = lax.dynamic_slice_in_dim(segments, first, qblock, 0)
            visible = visible_pairs(query_pos, query_seg, positions, segments)
            scores = jnp.einsum('tgd,sd->gts', q_rows, k_full) * score_scale
            masked = jnp.where(visible[None], scores, NEG)
            top = lax.optimization_barrier(jnp.max(masked, axis=-1))
            weights = jnp.where(visible[None], jnp.exp(masked - top[..., None]), 0.0)
            norm_sum = lax.optimization_barrier(jnp.sum(weights, axis=-1))
            log_sum = top + jnp.log(norm_sum)
            attn = jnp.einsum('gts,sd->tgd', rounded(weights), v_full) / norm_sum.T[..., None]
            attn_b = attn.astype(jnp.bfloat16)
            delta = lax.optimization_barrier(jnp.sum(rounded(attn) * d_rows, axis=-1)).T
            probs = jnp.where(visible[None], jnp.exp(masked - log_sum[..., None]), 0.0)
            value_grad = jnp.einsum('gts,tgd->sd', rounded(probs), d_rows)
            prob_grad = jnp.einsum('tgd,sd->gts', d_rows, v_full)
            score_grad = rounded(probs * (prob_grad - delta[..., None]))
            query_grad = jnp.einsum('gts,sd->tgd', score_grad, k_full) * score_scale
            key_grad = jnp.einsum('gts,tgd->sd', score_grad, q_rows) * score_scale
            return ((grads[0] + rounded(key_grad), grads[1] + rounded(value_grad)), (attn_b, query_grad.astype(jnp.bfloat16)))
        zeros = jnp.zeros((TOKENS, HD), jnp.float32)
        (key_sum, value_sum), (attn_blocks, query_blocks) = lax.scan(one_block, (zeros, zeros), jnp.arange(block_total, dtype=jnp.int32))
        return (attn_blocks.reshape(TOKENS, group_size, HD), query_blocks.reshape(TOKENS, group_size, HD), key_sum.astype(jnp.bfloat16), value_sum.astype(jnp.bfloat16))
    attn_all, grad_q, grad_k, grad_v = lax.map(one_head, (q_heads, k_heads, v_heads, d_heads))
    attn_rows = attn_all.transpose(1, 0, 2, 3).reshape(TOKENS, H * HD)
    group_rows = H * HD // N_KV
    y_total = jnp.zeros((TOKENS, D), jnp.float32)
    for group in range(N_KV):
        part_rows = attn_rows[:, group * group_rows:(group + 1) * group_rows]
        part_weight = w_out[group * group_rows:(group + 1) * group_rows]
        y_total = y_total + rounded(jnp.dot(part_rows, part_weight, preferred_element_type=jnp.float32))
    y_out = y_total.astype(jnp.bfloat16)
    grad_q = grad_q.transpose(1, 0, 2, 3).reshape(TOKENS, H * HD)
    grad_k = grad_k.transpose(1, 0, 2).reshape(TOKENS, KVH * HD)
    grad_v = grad_v.transpose(1, 0, 2).reshape(TOKENS, KVH * HD)
    return (y_out, grad_q, grad_k, grad_v)
```

```python
import functools
import math

import jax
import jax.numpy as jnp
from jax import lax
from jax.experimental import pallas as pl
from jax.experimental.pallas import tpu as pltpu
from jax.sharding import Mesh, PartitionSpec as P

H = 40
KVH = 8
HD = 128
BLK = 128
NRESP = 4
G = H // KVH
KB = 256
NEG = -1e30
SCALE = 1.0 / math.sqrt(HD)
C2 = SCALE * math.log2(math.e)
NT = (((1,), (1,)), ((), ()))
NN = (((1,), (0,)), ((), ()))


def dot(a, b, dims=NN):
    return lax.dot_general(a, b, dims, preferred_element_type=jnp.float32)


def seg_start(info, pos, prompt):
    start = jnp.where(pos >= info[1], info[1], prompt)
    start = jnp.where(pos >= info[2], info[2], start)
    return jnp.where(pos >= info[3], info[3], start)


def block_range(info, q_first, q_rows, prompt):
    full = jnp.minimum(prompt, q_first + 1) // KB
    first = jnp.where(q_first >= prompt, seg_start(info, q_first, prompt) // KB, full)
    last = (q_first + q_rows - 1) // KB + 1
    return full, first, last


def visible(info, q_first, q_rows, k_first, prompt):
    q_pos = q_first + lax.broadcasted_iota(jnp.int32, (1, q_rows), 1)
    start = seg_start(info, q_pos, prompt)
    k_pos = k_first + lax.broadcasted_iota(jnp.int32, (KB, q_rows), 0)
    return (k_pos <= q_pos) & ((k_pos < prompt) | (k_pos >= start))


def read_info(info_ref):
    return [info_ref[i] for i in range(4)]


def fwd_kernel(prompt, qb, info_ref, q_ref, k_ref, vt_ref, o_ref, lse_ref, m_ref, l_ref, acc_ref):
    info = read_info(info_ref)
    blocks = q_ref.shape[0] // qb

    def query_block(i, carry):
        rows = pl.ds(pl.multiple_of(i * qb, qb), qb)
        q_first = info[0] + i * qb
        m_ref[...] = jnp.full_like(m_ref, NEG)
        l_ref[...] = jnp.zeros_like(l_ref)
        acc_ref[...] = jnp.zeros_like(acc_ref)
        full, first, last = block_range(info, q_first, qb, prompt)

        def key_block(masked, b, carry):
            keys = pl.ds(pl.multiple_of(b * KB, KB), KB)
            k_blk = k_ref[keys, :]
            vt_blk = vt_ref[:, keys]
            vis = visible(info, q_first, qb, b * KB, prompt) if masked else None
            for h in range(G):
                s = dot(k_blk, q_ref[rows, h * HD:(h + 1) * HD], NT) * C2
                if masked:
                    s = jnp.where(vis, s, NEG)
                m_old = m_ref[h:h + 1, :]
                m_new = jnp.maximum(m_old, jnp.max(s, axis=0, keepdims=True))
                p = jnp.exp2(s - m_new)
                alpha = jnp.exp2(m_old - m_new)
                m_ref[h:h + 1, :] = m_new
                l_ref[h:h + 1, :] = l_ref[h:h + 1, :] * alpha + jnp.sum(p, axis=0, keepdims=True)
                acc_ref[h] = acc_ref[h] * alpha + dot(vt_blk, p.astype(jnp.bfloat16))
            return carry

        lax.fori_loop(0, full, functools.partial(key_block, False), 0)
        lax.fori_loop(first, last, functools.partial(key_block, True), 0)
        for h in range(G):
            l = l_ref[h:h + 1, :]
            o_ref[rows, h * HD:(h + 1) * HD] = (acc_ref[h] / l).T.astype(jnp.bfloat16)
            lse_ref[i, h:h + 1, :] = m_ref[h:h + 1, :] + jnp.log2(l)
        return carry

    lax.fori_loop(0, blocks, query_block, 0)


def bwd_kernel(prompt, qb, info_ref, q_ref, k_ref, kt_ref, v_ref, o_ref, lse_ref, do_ref,
               dq_ref, dkv_ref, qs_ref, dos_ref, del_ref, p_ref, ds_ref, dqt_ref, dk_ref, dv_ref):
    info = read_info(info_ref)
    blocks = q_ref.shape[0] // qb
    dk_ref[...] = jnp.zeros_like(dk_ref)
    dv_ref[...] = jnp.zeros_like(dv_ref)

    def query_block(i, carry):
        rows = pl.ds(pl.multiple_of(i * qb, qb), qb)
        q_first = info[0] + i * qb
        for h in range(G):
            cols = slice(h * HD, (h + 1) * HD)
            do = do_ref[rows, cols]
            qs_ref[h * qb:(h + 1) * qb, :] = q_ref[rows, cols]
            dos_ref[h * qb:(h + 1) * qb, :] = do
            prod = do.astype(jnp.float32) * o_ref[rows, cols].astype(jnp.float32)
            del_ref[h:h + 1, :] = jnp.sum(prod.T, axis=0, keepdims=True)
        dqt_ref[...] = jnp.zeros_like(dqt_ref)
        full, first, last = block_range(info, q_first, qb, prompt)

        def key_block(masked, b, carry):
            keys = pl.ds(pl.multiple_of(b * KB, KB), KB)
            k_blk = k_ref[keys, :]
            v_blk = v_ref[keys, :]
            vis = visible(info, q_first, qb, b * KB, prompt) if masked else None
            for h in range(G):
                part = slice(h * qb, (h + 1) * qb)
                s = dot(k_blk, qs_ref[part, :], NT) * C2
                p = jnp.exp2(s - lse_ref[i, h:h + 1, :])
                if masked:
                    p = jnp.where(vis, p, 0.0)
                dp = dot(v_blk, dos_ref[part, :], NT)
                p_ref[h] = p.astype(jnp.bfloat16)
                ds_ref[h] = (p * (dp - del_ref[h:h + 1, :])).astype(jnp.bfloat16)
            dv = jnp.zeros((KB, HD), jnp.float32)
            dk = jnp.zeros((KB, HD), jnp.float32)
            for h in range(G):
                part = slice(h * qb, (h + 1) * qb)
                dv += dot(p_ref[h], dos_ref[part, :])
                dk += dot(ds_ref[h], qs_ref[part, :])
                dqt_ref[h] += dot(kt_ref[:, keys], ds_ref[h])
            dv_ref[keys, :] += dv
            dk_ref[keys, :] += dk
            return carry

        lax.fori_loop(0, full, functools.partial(key_block, False), 0)
        lax.fori_loop(first, last, functools.partial(key_block, True), 0)
        for h in range(G):
            dq_ref[rows, h * HD:(h + 1) * HD] = (dqt_ref[h] * SCALE).T.astype(jnp.bfloat16)
        return carry

    lax.fori_loop(0, blocks, query_block, 0)
    dkv_ref[:, :HD] = (dk_ref[...] * SCALE).astype(jnp.bfloat16)
    dkv_ref[:, HD:] = dv_ref[...].astype(jnp.bfloat16)


VM = pl.BlockSpec(memory_space=pltpu.VMEM)
SM = pl.BlockSpec(memory_space=pltpu.SMEM)


def fwd_attention(info, q, k, vt, prompt, qb):
    rows, keys = q.shape[0], k.shape[0]
    work = G * rows * keys
    return pl.pallas_call(
        functools.partial(fwd_kernel, prompt, qb),
        out_shape=(
            jax.ShapeDtypeStruct((rows, G * HD), jnp.bfloat16),
            jax.ShapeDtypeStruct((rows // qb, 8, qb), jnp.float32),
        ),
        in_specs=[SM, VM, VM, VM],
        out_specs=(VM, VM),
        scratch_shapes=[
            pltpu.VMEM((8, qb), jnp.float32),
            pltpu.VMEM((8, qb), jnp.float32),
            pltpu.VMEM((G, HD, qb), jnp.float32),
        ],
        compiler_params=pltpu.CompilerParams(vmem_limit_bytes=24 << 20),
        cost_estimate=pl.CostEstimate(flops=work * HD * 4 * 2, bytes_accessed=4 << 20, transcendentals=work),
        name="attention_fwd",
    )(info, q, k, vt)


def bwd_attention(info, q, k, kt, v, o, lse, do, prompt, qb):
    rows, keys = q.shape[0], k.shape[0]
    work = G * rows * keys
    return pl.pallas_call(
        functools.partial(bwd_kernel, prompt, qb),
        out_shape=(
            jax.ShapeDtypeStruct((rows, G * HD), jnp.bfloat16),
            jax.ShapeDtypeStruct((keys, 2 * HD), jnp.bfloat16),
        ),
        in_specs=[SM] + [VM] * 7,
        out_specs=(VM, VM),
        scratch_shapes=[
            pltpu.VMEM((G * qb, HD), jnp.bfloat16),
            pltpu.VMEM((G * qb, HD), jnp.bfloat16),
            pltpu.VMEM((8, qb), jnp.float32),
            pltpu.VMEM((G, KB, qb), jnp.bfloat16),
            pltpu.VMEM((G, KB, qb), jnp.bfloat16),
            pltpu.VMEM((G, HD, qb), jnp.float32),
            pltpu.VMEM((keys, HD), jnp.float32),
            pltpu.VMEM((keys, HD), jnp.float32),
        ],
        compiler_params=pltpu.CompilerParams(vmem_limit_bytes=32 << 20),
        cost_estimate=pl.CostEstimate(flops=work * HD * 10 * 2, bytes_accessed=8 << 20, transcendentals=work),
        name="attention_bwd",
    )(info, q, k, kt, v, o, lse, do)


def local(queries, keys, values, w_out, grad_y, resp_blocks):
    heads = lax.axis_size("hd")
    tok = queries.shape[0]
    rows = tok * heads
    total = rows * lax.axis_size("tg")
    prompt = total // 2
    qb = 256 if rows % 256 == 0 else rows
    first = lax.axis_index("tg").astype(jnp.int32) * rows
    ends = prompt + jnp.cumsum(resp_blocks[: NRESP - 1]).astype(jnp.int32) * BLK
    info = jnp.concatenate([first[None], ends])

    def a2a(x, split, concat):
        return lax.all_to_all(x, "hd", split, concat, tiled=True) if heads > 1 else x

    kv = jnp.concatenate([keys.reshape(tok, heads, HD), values.reshape(tok, heads, HD)], axis=2)
    kv = a2a(kv.reshape(tok, heads * 2 * HD), 1, 0)
    kv = lax.all_gather(kv, "tg", axis=0, tiled=True)
    q = a2a(queries, 1, 0)
    wt = a2a(w_out.T, 1, 0)
    wt = lax.all_gather(wt, "tg", axis=0, tiled=True)
    gy = lax.all_gather(grad_y, "kv", axis=1, tiled=True)
    gy = lax.all_gather(gy, "hd", axis=0, tiled=True)
    k, v = kv[:, :HD], kv[:, HD:]
    attn, lse = fwd_attention(info, q, k, v.T, prompt, qb)
    grad_attn = jnp.dot(gy, wt, preferred_element_type=jnp.float32).astype(jnp.bfloat16)
    y = dot(attn, wt, NT).astype(jnp.bfloat16)
    y = lax.psum_scatter(y, "hd", scatter_dimension=0, tiled=True)
    y = lax.psum_scatter(y, "kv", scatter_dimension=1, tiled=True)
    dq, dkv = bwd_attention(info, q, k, k.T, v, attn, lse, grad_attn, prompt, qb)
    dkv = lax.psum_scatter(dkv, "tg", scatter_dimension=0, tiled=True)
    dkv = a2a(dkv, 0, 1).reshape(tok, heads, 2, HD)
    dq = a2a(dq, 0, 1)
    return (y, dq, dkv[:, :, 0].reshape(tok, heads * HD), dkv[:, :, 1].reshape(tok, heads * HD))


def solution(mesh):
    ctx, n_kv = mesh.devices.shape
    heads = KVH // n_kv
    split = Mesh(mesh.devices.reshape(ctx // heads, heads, n_kv), ("tg", "hd", "kv"))
    tok = ("tg", "hd")
    tiled = P(tok, "kv")
    return jax.shard_map(
        local,
        mesh=split,
        in_specs=(tiled, tiled, tiled, P("kv", tok), tiled, P()),
        out_specs=(tiled,) * 4,
        check_vma=False,
    )
```

```python
import functools
import math

import jax
import jax.numpy as jnp
from jax import lax
from jax.experimental import pallas as pl
from jax.experimental.pallas import tpu as pltpu
from jax.sharding import Mesh, PartitionSpec as P

H = 40
KVH = 8
HD = 128
BLK = 128
NRESP = 4
G = H // KVH
KB = 256
NEG = -1e30
SCALE = 1.0 / math.sqrt(HD)
C2 = SCALE * math.log2(math.e)
NT = (((1,), (1,)), ((), ()))
NN = (((1,), (0,)), ((), ()))


def dot(a, b, dims=NN):
    return lax.dot_general(a, b, dims, preferred_element_type=jnp.float32)


def seg_start(info, pos, prompt):
    start = jnp.where(pos >= info[1], info[1], prompt)
    start = jnp.where(pos >= info[2], info[2], start)
    return jnp.where(pos >= info[3], info[3], start)


def block_range(q_first, q_rows, prompt):
    full = jnp.minimum(prompt, q_first + 1) // KB
    return full, (q_first + q_rows - 1) // KB + 1


def visible(info, q_first, q_rows, k_first, prompt):
    q_pos = q_first + lax.broadcasted_iota(jnp.int32, (1, q_rows), 1)
    start = seg_start(info, q_pos, prompt)
    k_pos = k_first + lax.broadcasted_iota(jnp.int32, (KB, q_rows), 0)
    return (k_pos <= q_pos) & ((k_pos < prompt) | (k_pos >= start))


def place():
    me = lax.axis_index("tg"), lax.axis_index("hd"), lax.axis_index("kv")
    return [x.astype(jnp.int32) for x in me]


def sizes():
    return lax.axis_size("tg"), lax.axis_size("hd"), lax.axis_size("kv")


def span(index, size):
    return pl.ds(pl.multiple_of(index * size, size), size)


def remote(src, dst, sems, slot, target):
    return pltpu.make_async_remote_copy(
        src_ref=src,
        dst_ref=dst,
        send_sem=sems.at[0, slot],
        recv_sem=sems.at[1, slot],
        device_id=target,
        device_id_type=pl.DeviceIdType.MESH,
    )


def greet():
    t, i, k = place()
    tg, hd, kv = sizes()
    barrier = pltpu.get_barrier_semaphore()
    c = t * hd + i
    for d in range(1, tg * hd):
        p = lax.rem(c + d, tg * hd)
        pl.semaphore_signal(barrier, inc=1, device_id=(p // hd, lax.rem(p, hd), k), device_id_type=pl.DeviceIdType.MESH)
    for e in range(1, kv):
        for j in range(hd):
            pl.semaphore_signal(
                barrier, inc=1, device_id=(t, lax.rem(i + j, hd), lax.rem(k + e, kv)), device_id_type=pl.DeviceIdType.MESH
            )
    pl.semaphore_wait(barrier, tg * hd - 1 + (kv - 1) * hd)


def plane_peer(d):
    t, i, k = place()
    _, hd, kv = sizes()
    share = 2 if hd % 2 == 0 else 1
    chips = hd // share
    core = lax.rem(i, share)
    p = lax.rem(k * chips + i // share + d + chips * kv, chips * kv)
    return lax.rem(p, chips) * share + core, p // chips


def gather_kernel(prompt, qb, info_ref, kv_ref, q_ref, wt_ref, gy_ref,
                  kvall_ref, qall_ref, wtall_ref, gyall_ref, o_ref, lse_ref,
                  vt_ref, m_ref, l_ref, acc_ref, kv_sem, q_sem, w_sem, g_sem, f_sem, own_sem):
    t, i, k = place()
    tg, hd, n_kv = sizes()
    tok = q_ref.shape[0]
    wide = q_ref.shape[1]
    wrows = wt_ref.shape[0]
    n = tg * hd
    c = t * hd + i
    share = 2 if hd % 2 == 0 else 1
    ring = hd // share * n_kv
    greet()

    def at(p):
        return p // hd, lax.rem(p, hd)

    own = [
        pltpu.make_async_copy(kv_ref.at[:, span(i, 2 * HD)], kvall_ref.at[span(c, tok), :], own_sem.at[0]),
        pltpu.make_async_copy(q_ref.at[:, span(i, G * HD)], qall_ref.at[span(i, tok), :], own_sem.at[1]),
        pltpu.make_async_copy(wt_ref.at[:, span(i, G * HD)], wtall_ref.at[span(c, wrows), :], own_sem.at[2]),
        pltpu.make_async_copy(gy_ref, gyall_ref.at[span(i, tok), span(k, wide)], own_sem.at[3]),
    ]
    for copy in own:
        copy.start()

    def kv_copy(d, to):
        tt, ii = at(lax.rem(c + d, n))
        src = c if to else lax.rem(c - d + n, n)
        return remote(kv_ref.at[:, span(ii, 2 * HD)], kvall_ref.at[span(src, tok), :], kv_sem, d, (tt, ii, k))

    def q_copy(d, to):
        ii = lax.rem(i + d, hd)
        src = i if to else lax.rem(i - d + hd, hd)
        return remote(q_ref.at[:, span(ii, G * HD)], qall_ref.at[span(src, tok), :], q_sem, d, (t, ii, k))

    def w_copy(d, to):
        tt, ii = at(lax.rem(c + d, n))
        src = c if to else lax.rem(c - d + n, n)
        return remote(wt_ref.at[:, span(ii, G * HD)], wtall_ref.at[span(src, wrows), :], w_sem, d, (tt, ii, k))

    def g_copy(d, to):
        ii, kk = plane_peer(d)
        si, sk = (i, k) if to else plane_peer(-d)
        return remote(gy_ref, gyall_ref.at[span(si, tok), span(sk, wide)], g_sem, d, (t, ii, kk))

    def f_copy(d, to):
        si, sk = plane_peer(-d)
        if not to:
            si = si + 1 - 2 * lax.rem(si, 2)
        block = gyall_ref.at[span(si, tok), span(sk, wide)]
        return remote(gy_ref if d == 0 else block, block, f_sem, d, (t, i + 1 - 2 * lax.rem(i, 2), k))

    for d in range(1, n):
        kv_copy(d, True).start()
    for d in range(1, hd):
        q_copy(d, True).start()
    for d in range(1, ring):
        g_copy(d, True).start()
    if share == 2:
        f_copy(0, True).start()
    for d in range(1, n):
        w_copy(d, True).start()

    own[0].wait()
    own[1].wait()
    for d in range(1, n):
        kv_copy(d, False).wait_recv()
    for d in range(1, hd):
        q_copy(d, False).wait_recv()

    def turn(b, carry):
        keys = span(b, KB)
        vt_ref[:, keys] = kvall_ref[keys, HD:].T
        return carry

    lax.fori_loop(0, kvall_ref.shape[0] // KB, turn, 0)
    fwd_body(prompt, qb, info_ref, qall_ref, kvall_ref, vt_ref, o_ref, lse_ref, m_ref, l_ref, acc_ref)

    for d in range(1, ring):
        g_copy(d, False).wait_recv()
        if share == 2:
            f_copy(d, True).start()
    for d in range(1, n):
        w_copy(d, False).wait_recv()
    if share == 2:
        for d in range(ring):
            f_copy(d, False).wait_recv()
            f_copy(d, True).wait_send()
    for d in range(1, n):
        kv_copy(d, True).wait_send()
        w_copy(d, True).wait_send()
    for d in range(1, hd):
        q_copy(d, True).wait_send()
    for d in range(1, ring):
        g_copy(d, True).wait_send()
    own[2].wait()
    own[3].wait()


def scatter_kernel(prompt, qb, info_ref, y_ref, q_ref, kv_ref, o_ref, lse_ref, do_ref,
                   yout_ref, dqout_ref, dkout_ref, dvout_ref,
                   pair_ref, yin_ref, dq_ref, dkv_ref, dkvin_ref, kt_ref, qs_ref, dos_ref, del_ref, p_ref, ds_ref,
                   dqt_ref, dk_ref, dv_ref, pair_sem, y_sem, dq_sem, dkv_sem, own_sem):
    t, i, k = place()
    tg, hd, n_kv = sizes()
    tok, wide = yout_ref.shape
    n = tg * hd
    c = t * hd + i
    share = 2 if hd % 2 == 0 else 1
    ring = hd // share * n_kv
    greet()
    other = i + 1 - 2 * lax.rem(i, 2)

    def pair_copy(d):
        ii, kk = plane_peer(d)
        ii = ii + 1 - 2 * lax.rem(ii, 2)
        return remote(y_ref.at[span(ii, tok), span(kk, wide)], pair_ref.at[d], pair_sem, d, (t, other, k))

    def y_copy(d):
        ii, kk = plane_peer(d)
        src = pair_ref.at[d] if share == 2 else y_ref.at[span(ii, tok), span(kk, wide)]
        return remote(src, yin_ref.at[d], y_sem, d, (t, ii, kk))

    if share == 2:
        for d in range(ring):
            pair_copy(d).start()
    else:
        for d in range(1, ring):
            y_copy(d).start()

    def turn(b, carry):
        keys = span(b, KB)
        kt_ref[:, keys] = kv_ref[keys, :HD].T
        return carry

    lax.fori_loop(0, kv_ref.shape[0] // KB, turn, 0)

    if share == 2:
        for d in [*range(1, ring), 0]:
            pair_copy(d).wait_recv()
            ii, kk = plane_peer(d)

            def add(r, carry):
                rows = span(r, 16)
                mine = y_ref[pl.ds(pl.multiple_of(ii * tok + r * 16, 16), 16), span(kk, wide)]
                pair_ref[d, rows, :] = (pair_ref[d, rows, :].astype(jnp.float32) + mine.astype(jnp.float32)).astype(jnp.bfloat16)
                return carry

            lax.fori_loop(0, tok // 16, add, 0)
            if d:
                y_copy(d).start()

    bwd_body(prompt, qb, info_ref, q_ref, kv_ref, kt_ref, o_ref, lse_ref, do_ref,
             dq_ref, dkv_ref, qs_ref, dos_ref, del_ref, p_ref, ds_ref, dqt_ref, dk_ref, dv_ref)

    def dkv_copy(d, to):
        p = lax.rem(c + d, n)
        src = c if to else lax.rem(c - d + n, n)
        return remote(dkv_ref.at[span(p, tok), :], dkvin_ref.at[src], dkv_sem, d, (p // hd, lax.rem(p, hd), k))

    def dq_copy(d, to):
        ii = lax.rem(i + d, hd)
        src = i if to else lax.rem(i - d + hd, hd)
        return remote(dq_ref.at[span(ii, tok), :], dqout_ref.at[:, span(src, G * HD)], dq_sem, d, (t, ii, k))

    for d in range(1, n):
        dkv_copy(d, True).start()
    for d in range(1, hd):
        dq_copy(d, True).start()
    own = [
        pltpu.make_async_copy(dkv_ref.at[span(c, tok), :], dkvin_ref.at[c], own_sem.at[0]),
        pltpu.make_async_copy(dq_ref.at[span(i, tok), :], dqout_ref.at[:, span(i, G * HD)], own_sem.at[1]),
    ]
    for copy in own:
        copy.start()

    for d in range(1, ring):
        y_copy(d).wait_recv()

    def y_sum(r, carry):
        rows = span(r, 16)
        if share == 2:
            total = pair_ref[0, rows, :].astype(jnp.float32)
        else:
            total = y_ref[pl.ds(pl.multiple_of(i * tok + r * 16, 16), 16), span(k, wide)].astype(jnp.float32)
        for d in range(1, ring):
            total += yin_ref[d, rows, :].astype(jnp.float32)
        yout_ref[rows, :] = total.astype(jnp.bfloat16)
        return carry

    lax.fori_loop(0, tok // 16, y_sum, 0)
    own[0].wait()
    own[1].wait()
    for d in range(1, n):
        dkv_copy(d, False).wait_recv()

    def kv_sum(r, carry):
        rows = span(r, 32)
        for j in range(hd):
            total = dkvin_ref[j, rows, :].astype(jnp.float32)
            for u in range(1, tg):
                total += dkvin_ref[u * hd + j, rows, :].astype(jnp.float32)
            cols = slice(j * HD, (j + 1) * HD)
            dkout_ref[rows, cols] = total[:, :HD].astype(jnp.bfloat16)
            dvout_ref[rows, cols] = total[:, HD:].astype(jnp.bfloat16)
        return carry

    lax.fori_loop(0, tok // 32, kv_sum, 0)
    for d in range(1, hd):
        dq_copy(d, False).wait_recv()
        dq_copy(d, True).wait_send()
    for d in range(1, n):
        dkv_copy(d, True).wait_send()
    for d in range(1, ring):
        y_copy(d).wait_send()
    if share == 2:
        for d in range(ring):
            pair_copy(d).wait_send()


def read_info(info_ref):
    return [info_ref[i] for i in range(4)]


def fwd_body(prompt, qb, info_ref, q_ref, kv_ref, vt_ref, o_ref, lse_ref, m_ref, l_ref, acc_ref):
    info = read_info(info_ref)
    first_row = lax.axis_index("tg").astype(jnp.int32) * q_ref.shape[0]
    blocks = q_ref.shape[0] // qb

    def query_block(i, carry):
        rows = pl.ds(pl.multiple_of(i * qb, qb), qb)
        q_first = first_row + i * qb
        m_ref[...] = jnp.full_like(m_ref, NEG)
        l_ref[...] = jnp.zeros_like(l_ref)
        acc_ref[...] = jnp.zeros_like(acc_ref)
        full, last = block_range(q_first, qb, prompt)

        def key_block(masked, b, carry):
            keys = pl.ds(pl.multiple_of(b * KB, KB), KB)
            k_blk = kv_ref[keys, :HD]
            vt_blk = vt_ref[:, keys]
            vis = visible(info, q_first, qb, b * KB, prompt) if masked else None
            for h in range(G):
                s = dot(k_blk, q_ref[rows, h * HD:(h + 1) * HD], NT) * C2
                if masked:
                    s = jnp.where(vis, s, NEG)
                m_old = m_ref[h:h + 1, :]
                m_new = jnp.maximum(m_old, jnp.max(s, axis=0, keepdims=True))
                p = jnp.exp2(s - m_new)
                alpha = jnp.exp2(m_old - m_new)
                m_ref[h:h + 1, :] = m_new
                l_ref[h:h + 1, :] = l_ref[h:h + 1, :] * alpha + jnp.sum(p, axis=0, keepdims=True)
                acc_ref[h] = acc_ref[h] * alpha + dot(vt_blk, p.astype(jnp.bfloat16))
            return carry

        lax.fori_loop(0, full, functools.partial(key_block, False), 0)
        lax.fori_loop(full, last, functools.partial(key_block, True), 0)
        for h in range(G):
            l = l_ref[h:h + 1, :]
            o_ref[rows, h * HD:(h + 1) * HD] = (acc_ref[h] / l).T.astype(jnp.bfloat16)
            lse_ref[i, h:h + 1, :] = m_ref[h:h + 1, :] + jnp.log2(l)
        return carry

    lax.fori_loop(0, blocks, query_block, 0)


def bwd_body(prompt, qb, info_ref, q_ref, kv_ref, kt_ref, o_ref, lse_ref, do_ref,
               dq_ref, dkv_ref, qs_ref, dos_ref, del_ref, p_ref, ds_ref, dqt_ref, dk_ref, dv_ref):
    info = read_info(info_ref)
    first_row = lax.axis_index("tg").astype(jnp.int32) * q_ref.shape[0]
    blocks = q_ref.shape[0] // qb
    dk_ref[...] = jnp.zeros_like(dk_ref)
    dv_ref[...] = jnp.zeros_like(dv_ref)

    def query_block(i, carry):
        rows = pl.ds(pl.multiple_of(i * qb, qb), qb)
        q_first = first_row + i * qb
        for h in range(G):
            cols = slice(h * HD, (h + 1) * HD)
            do = do_ref[rows, cols]
            qs_ref[h * qb:(h + 1) * qb, :] = q_ref[rows, cols]
            dos_ref[h * qb:(h + 1) * qb, :] = do
            prod = do.astype(jnp.float32) * o_ref[rows, cols].astype(jnp.float32)
            del_ref[h:h + 1, :] = jnp.sum(prod.T, axis=0, keepdims=True)
        dqt_ref[...] = jnp.zeros_like(dqt_ref)
        full, last = block_range(q_first, qb, prompt)

        def key_block(masked, b, carry):
            keys = pl.ds(pl.multiple_of(b * KB, KB), KB)
            k_blk = kv_ref[keys, :HD]
            v_blk = kv_ref[keys, HD:]
            vis = visible(info, q_first, qb, b * KB, prompt) if masked else None
            for h in range(G):
                part = slice(h * qb, (h + 1) * qb)
                s = dot(k_blk, qs_ref[part, :], NT) * C2
                p = jnp.exp2(s - lse_ref[i, h:h + 1, :])
                if masked:
                    p = jnp.where(vis, p, 0.0)
                dp = dot(v_blk, dos_ref[part, :], NT)
                p_ref[h] = p.astype(jnp.bfloat16)
                ds_ref[h] = (p * (dp - del_ref[h:h + 1, :])).astype(jnp.bfloat16)
            dv = jnp.zeros((KB, HD), jnp.float32)
            dk = jnp.zeros((KB, HD), jnp.float32)
            for h in range(G):
                part = slice(h * qb, (h + 1) * qb)
                dv += dot(p_ref[h], dos_ref[part, :])
                dk += dot(ds_ref[h], qs_ref[part, :])
                dqt_ref[h] += dot(kt_ref[:, keys], ds_ref[h])
            dv_ref[keys, :] += dv
            dk_ref[keys, :] += dk
            return carry

        lax.fori_loop(0, full, functools.partial(key_block, False), 0)
        lax.fori_loop(full, last, functools.partial(key_block, True), 0)
        for h in range(G):
            dq_ref[rows, h * HD:(h + 1) * HD] = (dqt_ref[h] * SCALE).T.astype(jnp.bfloat16)
        return carry

    lax.fori_loop(0, blocks, query_block, 0)
    dkv_ref[:, :HD] = (dk_ref[...] * SCALE).astype(jnp.bfloat16)
    dkv_ref[:, HD:] = dv_ref[...].astype(jnp.bfloat16)


VM = pl.BlockSpec(memory_space=pltpu.VMEM)
SM = pl.BlockSpec(memory_space=pltpu.SMEM)
ANY = pl.BlockSpec(memory_space=pl.ANY)
BF = jnp.bfloat16
F32 = jnp.float32


def dma(count):
    return pltpu.SemaphoreType.DMA((2, count))


def gather_and_forward(info, kv, q, wt, gy, prompt, qb):
    tg, hd, n_kv = sizes()
    tok, n = q.shape[0], tg * hd
    rows, keys = tok * hd, tok * n
    work = G * rows * keys
    shape = jax.ShapeDtypeStruct
    return pl.pallas_call(
        functools.partial(gather_kernel, prompt, qb),
        out_shape=(
            shape((keys, 2 * HD), BF),
            shape((rows, G * HD), BF),
            shape((wt.shape[0] * n, G * HD), BF),
            shape((rows, gy.shape[1] * n_kv), BF),
            shape((rows, G * HD), BF),
            shape((rows // qb, 8, qb), F32),
        ),
        in_specs=[SM, ANY, ANY, ANY, ANY],
        out_specs=(VM, VM, ANY, ANY, VM, VM),
        scratch_shapes=[
            pltpu.VMEM((HD, keys), BF),
            pltpu.VMEM((8, qb), F32),
            pltpu.VMEM((8, qb), F32),
            pltpu.VMEM((G, HD, qb), F32),
            dma(n), dma(hd), dma(n), dma(hd * n_kv), dma(hd * n_kv),
            pltpu.SemaphoreType.DMA((4,)),
        ],
        compiler_params=pltpu.CompilerParams(vmem_limit_bytes=40 << 20, collective_id=0, has_side_effects=True),
        cost_estimate=pl.CostEstimate(flops=work * HD * 4, bytes_accessed=32 << 20, transcendentals=work),
        name="gather_and_forward",
    )(info, kv, q, wt, gy)


def backward_and_scatter(info, y, q, kv, o, lse, do, tok, wide, prompt, qb):
    tg, hd, n_kv = sizes()
    n = tg * hd
    rows, keys = tok * hd, tok * n
    share = 2 if hd % 2 == 0 else 1
    ring = hd // share * n_kv
    work = G * rows * keys
    shape = jax.ShapeDtypeStruct
    return pl.pallas_call(
        functools.partial(scatter_kernel, prompt, qb),
        out_shape=(
            shape((tok, wide), BF),
            shape((tok, hd * G * HD), BF),
            shape((tok, hd * HD), BF),
            shape((tok, hd * HD), BF),
        ),
        in_specs=[SM] + [VM] * 6,
        out_specs=(VM,) * 4,
        scratch_shapes=[
            pltpu.VMEM((ring if share == 2 else 1, tok, wide), BF),
            pltpu.VMEM((ring, tok, wide), BF),
            pltpu.VMEM((rows, G * HD), BF),
            pltpu.VMEM((keys, 2 * HD), BF),
            pltpu.VMEM((n, tok, 2 * HD), BF),
            pltpu.VMEM((HD, keys), BF),
            pltpu.VMEM((G * qb, HD), BF),
            pltpu.VMEM((G * qb, HD), BF),
            pltpu.VMEM((8, qb), F32),
            pltpu.VMEM((G, KB, qb), BF),
            pltpu.VMEM((G, KB, qb), BF),
            pltpu.VMEM((G, HD, qb), F32),
            pltpu.VMEM((keys, HD), F32),
            pltpu.VMEM((keys, HD), F32),
            dma(ring), dma(ring), dma(hd), dma(n),
            pltpu.SemaphoreType.DMA((2,)),
        ],
        compiler_params=pltpu.CompilerParams(vmem_limit_bytes=56 << 20, collective_id=1, has_side_effects=True),
        cost_estimate=pl.CostEstimate(flops=work * HD * 10, bytes_accessed=32 << 20, transcendentals=work),
        name="backward_and_scatter",
    )(info, y, q, kv, o, lse, do)


def local(queries, keys, values, w_out, grad_y, resp_blocks):
    heads = lax.axis_size("hd")
    tok = queries.shape[0]
    rows = tok * heads
    prompt = rows * lax.axis_size("tg") // 2
    qb = 256 if rows % 256 == 0 else rows
    ends = prompt + jnp.cumsum(resp_blocks[: NRESP - 1]).astype(jnp.int32) * BLK
    info = jnp.concatenate([jnp.zeros((1,), jnp.int32), ends])
    kv = jnp.concatenate([keys.reshape(tok, heads, HD), values.reshape(tok, heads, HD)], axis=2)
    kv = kv.reshape(tok, heads * 2 * HD)
    kv_all, q, wt, gy, attn, lse = gather_and_forward(info, kv, queries, w_out.T, grad_y, prompt, qb)
    y = dot(attn, wt, NT).astype(BF)
    grad_attn = dot(gy, wt).astype(BF)
    return backward_and_scatter(info, y, q, kv_all, attn, lse, grad_attn, tok, grad_y.shape[1], prompt, qb)


def solution(mesh):
    ctx, n_kv = mesh.devices.shape
    heads = KVH // n_kv
    split = Mesh(mesh.devices.reshape(ctx // heads, heads, n_kv), ("tg", "hd", "kv"))
    tok = ("tg", "hd")
    tiled = P(tok, "kv")
    return jax.shard_map(
        local,
        mesh=split,
        in_specs=(tiled, tiled, tiled, P("kv", tok), tiled, P()),
        out_specs=(tiled,) * 4,
        check_vma=False,
    )
```

```python
import functools
import math

import jax
import jax.numpy as jnp
from jax import lax
from jax.experimental import pallas as pl
from jax.experimental.pallas import tpu as pltpu
from jax.sharding import Mesh, PartitionSpec as P

H = 40
KVH = 8
HD = 128
BLK = 128
NRESP = 4
G = H // KVH
KB = 256
NEG = -1e30
SCALE = 1.0 / math.sqrt(HD)
C2 = SCALE * math.log2(math.e)
NT = (((1,), (1,)), ((), ()))
NN = (((1,), (0,)), ((), ()))


def dot(a, b, dims=NN):
    return lax.dot_general(a, b, dims, preferred_element_type=jnp.float32)


def seg_start(info, pos, prompt):
    start = jnp.where(pos >= info[1], info[1], prompt)
    start = jnp.where(pos >= info[2], info[2], start)
    return jnp.where(pos >= info[3], info[3], start)


def block_range(q_first, q_rows, prompt):
    full = jnp.minimum(prompt, q_first + 1) // KB
    return full, (q_first + q_rows - 1) // KB + 1


def visible(info, q_first, q_rows, k_first, prompt):
    q_pos = q_first + lax.broadcasted_iota(jnp.int32, (1, q_rows), 1)
    start = seg_start(info, q_pos, prompt)
    k_pos = k_first + lax.broadcasted_iota(jnp.int32, (KB, q_rows), 0)
    return (k_pos <= q_pos) & ((k_pos < prompt) | (k_pos >= start))


def place():
    me = lax.axis_index("tg"), lax.axis_index("hd"), lax.axis_index("kv")
    return [x.astype(jnp.int32) for x in me]


def sizes():
    return lax.axis_size("tg"), lax.axis_size("hd"), lax.axis_size("kv")


def span(index, size):
    return pl.ds(pl.multiple_of(index * size, size), size)


def remote(src, dst, sems, slot, target):
    return pltpu.make_async_remote_copy(
        src_ref=src,
        dst_ref=dst,
        send_sem=sems.at[0, slot],
        recv_sem=sems.at[1, slot],
        device_id=target,
        device_id_type=pl.DeviceIdType.MESH,
    )


def greet():
    t, i, k = place()
    tg, hd, kv = sizes()
    barrier = pltpu.get_barrier_semaphore()
    c = t * hd + i
    for d in range(1, tg * hd):
        p = lax.rem(c + d, tg * hd)
        pl.semaphore_signal(barrier, inc=1, device_id=(p // hd, lax.rem(p, hd), k), device_id_type=pl.DeviceIdType.MESH)
    for e in range(1, kv):
        for j in range(hd):
            pl.semaphore_signal(
                barrier, inc=1, device_id=(t, lax.rem(i + j, hd), lax.rem(k + e, kv)), device_id_type=pl.DeviceIdType.MESH
            )
    pl.semaphore_wait(barrier, tg * hd - 1 + (kv - 1) * hd)


def plane_peer(d):
    t, i, k = place()
    _, hd, kv = sizes()
    share = 2 if hd % 2 == 0 else 1
    chips = hd // share
    core = lax.rem(i, share)
    p = lax.rem(k * chips + i // share + d + chips * kv, chips * kv)
    return lax.rem(p, chips) * share + core, p // chips


def gather_kernel(prompt, qb, info_ref, kv_ref, q_ref, wt_ref, gy_ref,
                  kvall_ref, qall_ref, o_ref, lse_ref, y_ref, do_ref,
                  wtall_ref, gyall_ref, ga_ref, vt_ref, m_ref, l_ref, acc_ref,
                  kv_sem, q_sem, w_sem, first_up, first_down, up_sem, down_sem, g_sem, f_sem, own_sem):
    t, i, k = place()
    tg, hd, n_kv = sizes()
    tok = q_ref.shape[0]
    wide = q_ref.shape[1]
    wrows = wt_ref.shape[0]
    n = tg * hd
    c = t * hd + i
    share = 2 if hd % 2 == 0 else 1
    ring = hd // share * n_kv
    greet()

    def at(p):
        return p // hd, lax.rem(p, hd)

    own = [
        pltpu.make_async_copy(kv_ref.at[:, span(i, 2 * HD)], kvall_ref.at[span(c, tok), :], own_sem.at[0]),
        pltpu.make_async_copy(q_ref.at[:, span(i, G * HD)], qall_ref.at[span(i, tok), :], own_sem.at[1]),
        pltpu.make_async_copy(wt_ref.at[:, span(i, G * HD)], wtall_ref.at[span(c, wrows), :], own_sem.at[2]),
        pltpu.make_async_copy(gy_ref, gyall_ref.at[span(i, tok), span(k, wide)], own_sem.at[3]),
    ]
    for copy in own:
        copy.start()

    def kv_copy(d, to):
        tt, ii = at(lax.rem(c + d, n))
        src = c if to else lax.rem(c - d + n, n)
        return remote(kv_ref.at[:, span(ii, 2 * HD)], kvall_ref.at[span(src, tok), :], kv_sem, d, (tt, ii, k))

    def q_copy(d, to):
        ii = lax.rem(i + d, hd)
        src = i if to else lax.rem(i - d + hd, hd)
        return remote(q_ref.at[:, span(ii, G * HD)], qall_ref.at[span(src, tok), :], q_sem, d, (t, ii, k))

    def w_copy(d, to):
        ii = lax.rem(i + d, hd)
        src = i if to else lax.rem(i - d + hd, hd)
        return remote(wt_ref.at[:, span(ii, G * HD)], wtall_ref.at[span(t * hd + src, wrows), :], w_sem, d, (t, ii, k))

    def first_hop(d, step, to):
        src = lax.rem(i - d + hd, hd)
        rows = span((t if to else t - step) * hd + src, wrows)
        block = wtall_ref.at[rows, :]
        out = wt_ref.at[:, span(i, G * HD)] if d == 0 else block
        return remote(out, block, first_up if step > 0 else first_down, d, (t + step, i, k))

    def hop(h, step, to):
        block = wtall_ref.at[span(t - step * (h if to else h + 1), wrows * hd), :]
        return remote(block, block, up_sem if step > 0 else down_sem, h, (t + step, i, k))

    def has(h, step):
        return t >= h if step > 0 else t + h < tg

    def more(step):
        return t < tg - 1 if step > 0 else t > 0

    def arrive_first():
        for step in (1, -1):
            @pl.when(has(1, step))
            def _():
                for d in range(hd):
                    first_hop(d, step, False).wait_recv()

            if tg > 2:
                @pl.when(has(1, step) & more(step))
                def _():
                    hop(1, step, True).start()

    def arrive(h):
        for step in (1, -1):
            @pl.when(has(h, step))
            def _():
                hop(h - 1, step, False).wait_recv()

            @pl.when(has(h, step) & more(step) & (h < tg - 1))
            def _():
                hop(h, step, True).start()

    part = wtall_ref.shape[0] // 4 if wrows * hd % HD else wrows * hd

    def project(u):
        cols = span(u, part)

        def tile(r, carry):
            rows = span(r, qb)
            w = wtall_ref[cols, :]
            ga_ref[rows, :] += dot(gyall_ref[rows, cols], w)
            y_ref[rows, cols] = dot(o_ref[rows, :], w, NT).astype(BF)
            return carry

        lax.fori_loop(0, o_ref.shape[0] // qb, tile, 0)

    def project_far(h):
        if wrows * hd % HD == 0:
            for step in (1, -1):
                @pl.when(has(h, step))
                def _():
                    project(t - step * h)

    def g_copy(d, to):
        ii, kk = plane_peer(d)
        si, sk = (i, k) if to else plane_peer(-d)
        return remote(gy_ref, gyall_ref.at[span(si, tok), span(sk, wide)], g_sem, d, (t, ii, kk))

    def f_copy(d, to):
        si, sk = plane_peer(-d)
        if not to:
            si = si + 1 - 2 * lax.rem(si, 2)
        block = gyall_ref.at[span(si, tok), span(sk, wide)]
        return remote(gy_ref if d == 0 else block, block, f_sem, d, (t, i + 1 - 2 * lax.rem(i, 2), k))

    for d in range(1, n):
        kv_copy(d, True).start()
    for d in range(1, hd):
        w_copy(d, True).start()
    for d in range(1, hd):
        q_copy(d, True).start()
    for step in (1, -1):
        @pl.when(more(step))
        def _():
            first_hop(0, step, True).start()
    for d in range(1, ring):
        g_copy(d, True).start()
    if share == 2:
        f_copy(0, True).start()
    for d in range(1, hd):
        w_copy(d, False).wait_recv()
        for step in (1, -1):
            @pl.when(more(step))
            def _():
                first_hop(d, step, True).start()

    ga_ref[...] = jnp.zeros_like(ga_ref)
    own[0].wait()
    own[1].wait()
    for d in range(1, n):
        kv_copy(d, False).wait_recv()
    for d in range(1, hd):
        q_copy(d, False).wait_recv()

    def turn(b, carry):
        keys = span(b, KB)
        vt_ref[:, keys] = kvall_ref[keys, HD:].T
        return carry

    lax.fori_loop(0, kvall_ref.shape[0] // KB, turn, 0)
    blocks = o_ref.shape[0] // qb
    fwd_body(prompt, qb, info_ref, qall_ref, kvall_ref, vt_ref, o_ref, lse_ref, m_ref, l_ref, acc_ref,
             arrive_first, max(blocks - 2, 0))

    for d in range(1, ring):
        g_copy(d, False).wait_recv()
        if share == 2:
            f_copy(d, True).start()
    if share == 2:
        for d in range(ring):
            f_copy(d, False).wait_recv()
    own[2].wait()
    own[3].wait()
    if wrows * hd % HD == 0:
        project(t)

    def step_far(h, carry):
        arrive(h + 1)
        project_far(h)
        return carry

    lax.fori_loop(1, tg - 1, step_far, 0)
    project_far(tg - 1)
    if wrows * hd % HD:
        lax.fori_loop(0, 4, lambda u, carry: (project(u), carry)[1], 0)
    do_ref[...] = ga_ref[...].astype(BF)

    if share == 2:
        for d in range(ring):
            f_copy(d, True).wait_send()
    for d in range(1, n):
        kv_copy(d, True).wait_send()
    for d in range(1, hd):
        w_copy(d, True).wait_send()
        q_copy(d, True).wait_send()
    for d in range(1, ring):
        g_copy(d, True).wait_send()
    for step in (1, -1):
        @pl.when(more(step))
        def _():
            for d in range(hd):
                first_hop(d, step, True).wait_send()

        def sent(h, carry):
            @pl.when(has(h, step) & more(step))
            def _():
                hop(h, step, True).wait_send()

            return carry

        lax.fori_loop(1, tg - 1, sent, 0)


def scatter_kernel(prompt, qb, info_ref, y_ref, q_ref, kv_ref, o_ref, lse_ref, do_ref,
                   yout_ref, dqout_ref, dkout_ref, dvout_ref,
                   pair_ref, yin_ref, dq_ref, dkv_ref, dkvin_ref, kt_ref, qs_ref, dos_ref, del_ref, p_ref, ds_ref,
                   dqt_ref, dk_ref, dv_ref, pair_sem, y_sem, dq_sem, dkv_sem, own_sem):
    t, i, k = place()
    tg, hd, n_kv = sizes()
    tok, wide = yout_ref.shape
    n = tg * hd
    c = t * hd + i
    share = 2 if hd % 2 == 0 else 1
    ring = hd // share * n_kv
    greet()
    other = i + 1 - 2 * lax.rem(i, 2)

    def pair_copy(d):
        ii, kk = plane_peer(d)
        ii = ii + 1 - 2 * lax.rem(ii, 2)
        return remote(y_ref.at[span(ii, tok), span(kk, wide)], pair_ref.at[d], pair_sem, d, (t, other, k))

    def y_copy(d):
        ii, kk = plane_peer(d)
        src = pair_ref.at[d] if share == 2 else y_ref.at[span(ii, tok), span(kk, wide)]
        return remote(src, yin_ref.at[d], y_sem, d, (t, ii, kk))

    if share == 2:
        for d in range(ring):
            pair_copy(d).start()
    else:
        for d in range(1, ring):
            y_copy(d).start()

    def turn(b, carry):
        keys = span(b, KB)
        kt_ref[:, keys] = kv_ref[keys, :HD].T
        return carry

    lax.fori_loop(0, kv_ref.shape[0] // KB, turn, 0)

    if share == 2:
        for d in [*range(1, ring), 0]:
            pair_copy(d).wait_recv()
            ii, kk = plane_peer(d)

            def add(r, carry):
                rows = span(r, 16)
                mine = y_ref[pl.ds(pl.multiple_of(ii * tok + r * 16, 16), 16), span(kk, wide)]
                pair_ref[d, rows, :] = (pair_ref[d, rows, :].astype(jnp.float32) + mine.astype(jnp.float32)).astype(jnp.bfloat16)
                return carry

            lax.fori_loop(0, tok // 16, add, 0)
            if d:
                y_copy(d).start()

    bwd_body(prompt, qb, info_ref, q_ref, kv_ref, kt_ref, o_ref, lse_ref, do_ref,
             dq_ref, dkv_ref, qs_ref, dos_ref, del_ref, p_ref, ds_ref, dqt_ref, dk_ref, dv_ref)

    def dkv_copy(d, to):
        p = lax.rem(c + d, n)
        src = c if to else lax.rem(c - d + n, n)
        return remote(dkv_ref.at[span(p, tok), :], dkvin_ref.at[src], dkv_sem, d, (p // hd, lax.rem(p, hd), k))

    def dq_copy(d, to):
        ii = lax.rem(i + d, hd)
        src = i if to else lax.rem(i - d + hd, hd)
        return remote(dq_ref.at[span(ii, tok), :], dqout_ref.at[:, span(src, G * HD)], dq_sem, d, (t, ii, k))

    for d in range(1, n):
        dkv_copy(d, True).start()
    for d in range(1, hd):
        dq_copy(d, True).start()
    own = [
        pltpu.make_async_copy(dkv_ref.at[span(c, tok), :], dkvin_ref.at[c], own_sem.at[0]),
        pltpu.make_async_copy(dq_ref.at[span(i, tok), :], dqout_ref.at[:, span(i, G * HD)], own_sem.at[1]),
    ]
    for copy in own:
        copy.start()

    for d in range(1, ring):
        y_copy(d).wait_recv()

    def y_sum(r, carry):
        rows = span(r, 16)
        if share == 2:
            total = pair_ref[0, rows, :].astype(jnp.float32)
        else:
            total = y_ref[pl.ds(pl.multiple_of(i * tok + r * 16, 16), 16), span(k, wide)].astype(jnp.float32)
        for d in range(1, ring):
            total += yin_ref[d, rows, :].astype(jnp.float32)
        yout_ref[rows, :] = total.astype(jnp.bfloat16)
        return carry

    lax.fori_loop(0, tok // 16, y_sum, 0)
    own[0].wait()
    own[1].wait()
    for d in range(1, n):
        dkv_copy(d, False).wait_recv()

    def kv_sum(r, carry):
        rows = span(r, 32)
        for j in range(hd):
            total = dkvin_ref[j, rows, :].astype(jnp.float32)
            for u in range(1, tg):
                total += dkvin_ref[u * hd + j, rows, :].astype(jnp.float32)
            cols = slice(j * HD, (j + 1) * HD)
            dkout_ref[rows, cols] = total[:, :HD].astype(jnp.bfloat16)
            dvout_ref[rows, cols] = total[:, HD:].astype(jnp.bfloat16)
        return carry

    lax.fori_loop(0, tok // 32, kv_sum, 0)
    for d in range(1, hd):
        dq_copy(d, False).wait_recv()
        dq_copy(d, True).wait_send()
    for d in range(1, n):
        dkv_copy(d, True).wait_send()
    for d in range(1, ring):
        y_copy(d).wait_send()
    if share == 2:
        for d in range(ring):
            pair_copy(d).wait_send()


def read_info(info_ref):
    return [info_ref[i] for i in range(4)]


def fwd_body(prompt, qb, info_ref, q_ref, kv_ref, vt_ref, o_ref, lse_ref, m_ref, l_ref, acc_ref, between, after):
    info = read_info(info_ref)
    first_row = lax.axis_index("tg").astype(jnp.int32) * q_ref.shape[0]
    blocks = q_ref.shape[0] // qb

    def query_block(i, carry):
        rows = pl.ds(pl.multiple_of(i * qb, qb), qb)
        q_first = first_row + i * qb
        m_ref[...] = jnp.full_like(m_ref, NEG)
        l_ref[...] = jnp.zeros_like(l_ref)
        acc_ref[...] = jnp.zeros_like(acc_ref)
        full, last = block_range(q_first, qb, prompt)

        def key_block(masked, b, carry):
            keys = pl.ds(pl.multiple_of(b * KB, KB), KB)
            k_blk = kv_ref[keys, :HD]
            vt_blk = vt_ref[:, keys]
            vis = visible(info, q_first, qb, b * KB, prompt) if masked else None
            for h in range(G):
                s = dot(k_blk, q_ref[rows, h * HD:(h + 1) * HD], NT) * C2
                if masked:
                    s = jnp.where(vis, s, NEG)
                m_old = m_ref[h:h + 1, :]
                m_new = jnp.maximum(m_old, jnp.max(s, axis=0, keepdims=True))
                p = jnp.exp2(s - m_new)
                alpha = jnp.exp2(m_old - m_new)
                m_ref[h:h + 1, :] = m_new
                l_ref[h:h + 1, :] = l_ref[h:h + 1, :] * alpha + jnp.sum(p, axis=0, keepdims=True)
                acc_ref[h] = acc_ref[h] * alpha + dot(vt_blk, p.astype(jnp.bfloat16))
            return carry

        lax.fori_loop(0, full, functools.partial(key_block, False), 0)
        lax.fori_loop(full, last, functools.partial(key_block, True), 0)
        for h in range(G):
            l = l_ref[h:h + 1, :]
            o_ref[rows, h * HD:(h + 1) * HD] = (acc_ref[h] / l).T.astype(jnp.bfloat16)
            lse_ref[i, h:h + 1, :] = m_ref[h:h + 1, :] + jnp.log2(l)
        pl.when(i == after)(between)
        return carry

    lax.fori_loop(0, blocks, query_block, 0)


def bwd_body(prompt, qb, info_ref, q_ref, kv_ref, kt_ref, o_ref, lse_ref, do_ref,
               dq_ref, dkv_ref, qs_ref, dos_ref, del_ref, p_ref, ds_ref, dqt_ref, dk_ref, dv_ref):
    info = read_info(info_ref)
    first_row = lax.axis_index("tg").astype(jnp.int32) * q_ref.shape[0]
    blocks = q_ref.shape[0] // qb
    dk_ref[...] = jnp.zeros_like(dk_ref)
    dv_ref[...] = jnp.zeros_like(dv_ref)

    def query_block(i, carry):
        rows = pl.ds(pl.multiple_of(i * qb, qb), qb)
        q_first = first_row + i * qb
        for h in range(G):
            cols = slice(h * HD, (h + 1) * HD)
            do = do_ref[rows, cols]
            qs_ref[h * qb:(h + 1) * qb, :] = q_ref[rows, cols]
            dos_ref[h * qb:(h + 1) * qb, :] = do
            prod = do.astype(jnp.float32) * o_ref[rows, cols].astype(jnp.float32)
            del_ref[h:h + 1, :] = jnp.sum(prod.T, axis=0, keepdims=True)
        dqt_ref[...] = jnp.zeros_like(dqt_ref)
        full, last = block_range(q_first, qb, prompt)

        def key_block(masked, b, carry):
            keys = pl.ds(pl.multiple_of(b * KB, KB), KB)
            k_blk = kv_ref[keys, :HD]
            v_blk = kv_ref[keys, HD:]
            vis = visible(info, q_first, qb, b * KB, prompt) if masked else None
            for h in range(G):
                part = slice(h * qb, (h + 1) * qb)
                s = dot(k_blk, qs_ref[part, :], NT) * C2
                p = jnp.exp2(s - lse_ref[i, h:h + 1, :])
                if masked:
                    p = jnp.where(vis, p, 0.0)
                dp = dot(v_blk, dos_ref[part, :], NT)
                p_ref[h] = p.astype(jnp.bfloat16)
                ds_ref[h] = (p * (dp - del_ref[h:h + 1, :])).astype(jnp.bfloat16)
            dv = jnp.zeros((KB, HD), jnp.float32)
            dk = jnp.zeros((KB, HD), jnp.float32)
            for h in range(G):
                part = slice(h * qb, (h + 1) * qb)
                dv += dot(p_ref[h], dos_ref[part, :])
                dk += dot(ds_ref[h], qs_ref[part, :])
                dqt_ref[h] += dot(kt_ref[:, keys], ds_ref[h])
            dv_ref[keys, :] += dv
            dk_ref[keys, :] += dk
            return carry

        lax.fori_loop(0, full, functools.partial(key_block, False), 0)
        lax.fori_loop(full, last, functools.partial(key_block, True), 0)
        for h in range(G):
            dq_ref[rows, h * HD:(h + 1) * HD] = (dqt_ref[h] * SCALE).T.astype(jnp.bfloat16)
        return carry

    lax.fori_loop(0, blocks, query_block, 0)
    dkv_ref[:, :HD] = (dk_ref[...] * SCALE).astype(jnp.bfloat16)
    dkv_ref[:, HD:] = dv_ref[...].astype(jnp.bfloat16)


VM = pl.BlockSpec(memory_space=pltpu.VMEM)
SM = pl.BlockSpec(memory_space=pltpu.SMEM)
ANY = pl.BlockSpec(memory_space=pl.ANY)
BF = jnp.bfloat16
F32 = jnp.float32


def dma(count):
    return pltpu.SemaphoreType.DMA((2, count))


def gather_and_forward(info, kv, q, wt, gy, prompt, qb):
    tg, hd, n_kv = sizes()
    tok, n = q.shape[0], tg * hd
    rows, keys = tok * hd, tok * n
    work = G * rows * keys
    shape = jax.ShapeDtypeStruct
    return pl.pallas_call(
        functools.partial(gather_kernel, prompt, qb),
        out_shape=(
            shape((keys, 2 * HD), BF),
            shape((rows, G * HD), BF),
            shape((rows, G * HD), BF),
            shape((rows // qb, 8, qb), F32),
            shape((rows, gy.shape[1] * n_kv), BF),
            shape((rows, G * HD), BF),
        ),
        in_specs=[SM, ANY, ANY, ANY, ANY],
        out_specs=(VM,) * 6,
        scratch_shapes=[
            pltpu.VMEM((wt.shape[0] * n, G * HD), BF),
            pltpu.VMEM((rows, gy.shape[1] * n_kv), BF),
            pltpu.VMEM((rows, G * HD), F32),
            pltpu.VMEM((HD, keys), BF),
            pltpu.VMEM((8, qb), F32),
            pltpu.VMEM((8, qb), F32),
            pltpu.VMEM((G, HD, qb), F32),
            dma(n), dma(hd), dma(hd), dma(hd), dma(hd), dma(tg), dma(tg), dma(hd * n_kv), dma(hd * n_kv),
            pltpu.SemaphoreType.DMA((4,)),
        ],
        compiler_params=pltpu.CompilerParams(vmem_limit_bytes=56 << 20, collective_id=0, has_side_effects=True),
        cost_estimate=pl.CostEstimate(flops=work * HD * 4, bytes_accessed=32 << 20, transcendentals=work),
        name="gather_and_forward",
    )(info, kv, q, wt, gy)


def backward_and_scatter(info, y, q, kv, o, lse, do, tok, wide, prompt, qb):
    tg, hd, n_kv = sizes()
    n = tg * hd
    rows, keys = tok * hd, tok * n
    share = 2 if hd % 2 == 0 else 1
    ring = hd // share * n_kv
    work = G * rows * keys
    shape = jax.ShapeDtypeStruct
    return pl.pallas_call(
        functools.partial(scatter_kernel, prompt, qb),
        out_shape=(
            shape((tok, wide), BF),
            shape((tok, hd * G * HD), BF),
            shape((tok, hd * HD), BF),
            shape((tok, hd * HD), BF),
        ),
        in_specs=[SM] + [VM] * 6,
        out_specs=(VM,) * 4,
        scratch_shapes=[
            pltpu.VMEM((ring if share == 2 else 1, tok, wide), BF),
            pltpu.VMEM((ring, tok, wide), BF),
            pltpu.VMEM((rows, G * HD), BF),
            pltpu.VMEM((keys, 2 * HD), BF),
            pltpu.VMEM((n, tok, 2 * HD), BF),
            pltpu.VMEM((HD, keys), BF),
            pltpu.VMEM((G * qb, HD), BF),
            pltpu.VMEM((G * qb, HD), BF),
            pltpu.VMEM((8, qb), F32),
            pltpu.VMEM((G, KB, qb), BF),
            pltpu.VMEM((G, KB, qb), BF),
            pltpu.VMEM((G, HD, qb), F32),
            pltpu.VMEM((keys, HD), F32),
            pltpu.VMEM((keys, HD), F32),
            dma(ring), dma(ring), dma(hd), dma(n),
            pltpu.SemaphoreType.DMA((2,)),
        ],
        compiler_params=pltpu.CompilerParams(vmem_limit_bytes=56 << 20, collective_id=1, has_side_effects=True),
        cost_estimate=pl.CostEstimate(flops=work * HD * 10, bytes_accessed=32 << 20, transcendentals=work),
        name="backward_and_scatter",
    )(info, y, q, kv, o, lse, do)


def local(queries, keys, values, w_out, grad_y, resp_blocks):
    heads = lax.axis_size("hd")
    tok = queries.shape[0]
    rows = tok * heads
    prompt = rows * lax.axis_size("tg") // 2
    qb = 256 if rows % 256 == 0 else rows
    ends = prompt + jnp.cumsum(resp_blocks[: NRESP - 1]).astype(jnp.int32) * BLK
    info = jnp.concatenate([jnp.zeros((1,), jnp.int32), ends])
    kv = jnp.concatenate([keys.reshape(tok, heads, HD), values.reshape(tok, heads, HD)], axis=2)
    kv = kv.reshape(tok, heads * 2 * HD)
    kv_all, q, attn, lse, y, grad_attn = gather_and_forward(info, kv, queries, w_out.T, grad_y, prompt, qb)
    return backward_and_scatter(info, y, q, kv_all, attn, lse, grad_attn, tok, grad_y.shape[1], prompt, qb)


def solution(mesh):
    ctx, n_kv = mesh.devices.shape
    heads = KVH // n_kv
    split = Mesh(mesh.devices.reshape(ctx // heads, heads, n_kv), ("tg", "hd", "kv"))
    tok = ("tg", "hd")
    tiled = P(tok, "kv")
    return jax.shard_map(
        local,
        mesh=split,
        in_specs=(tiled, tiled, tiled, P("kv", tok), tiled, P()),
        out_specs=(tiled,) * 4,
        check_vma=False,
    )
```

```python
import functools
import math

import jax
import jax.numpy as jnp
from jax import lax
from jax.experimental import pallas as pl
from jax.experimental.pallas import tpu as pltpu
from jax.sharding import Mesh, PartitionSpec as P

H = 40
KVH = 8
HD = 128
BLK = 128
NRESP = 4
G = H // KVH
KB = 256
NEG = -1e30
SCALE = 1.0 / math.sqrt(HD)
C2 = SCALE * math.log2(math.e)
NT = (((1,), (1,)), ((), ()))
NN = (((1,), (0,)), ((), ()))


def dot(a, b, dims=NN):
    return lax.dot_general(a, b, dims, preferred_element_type=jnp.float32)


def seg_start(info, pos, prompt):
    start = jnp.where(pos >= info[1], info[1], prompt)
    start = jnp.where(pos >= info[2], info[2], start)
    return jnp.where(pos >= info[3], info[3], start)


def block_range(q_first, q_rows, prompt):
    full = jnp.minimum(prompt, q_first + 1) // KB
    return full, (q_first + q_rows - 1) // KB + 1


def visible(info, q_first, q_rows, k_first, prompt):
    q_pos = q_first + lax.broadcasted_iota(jnp.int32, (1, q_rows), 1)
    start = seg_start(info, q_pos, prompt)
    k_pos = k_first + lax.broadcasted_iota(jnp.int32, (KB, q_rows), 0)
    return (k_pos <= q_pos) & ((k_pos < prompt) | (k_pos >= start))


def place():
    me = lax.axis_index("tg"), lax.axis_index("hd"), lax.axis_index("kv")
    return [x.astype(jnp.int32) for x in me]


def sizes():
    return lax.axis_size("tg"), lax.axis_size("hd"), lax.axis_size("kv")


def span(index, size):
    return pl.ds(pl.multiple_of(index * size, size), size)


def remote(src, dst, sems, slot, target):
    return pltpu.make_async_remote_copy(
        src_ref=src,
        dst_ref=dst,
        send_sem=sems.at[0, slot],
        recv_sem=sems.at[1, slot],
        device_id=target,
        device_id_type=pl.DeviceIdType.MESH,
    )


def greet():
    t, i, k = place()
    tg, hd, kv = sizes()
    barrier = pltpu.get_barrier_semaphore()
    c = t * hd + i
    for d in range(1, tg * hd):
        p = lax.rem(c + d, tg * hd)
        pl.semaphore_signal(barrier, inc=1, device_id=(p // hd, lax.rem(p, hd), k), device_id_type=pl.DeviceIdType.MESH)
    for e in range(1, kv):
        for j in range(hd):
            pl.semaphore_signal(
                barrier, inc=1, device_id=(t, lax.rem(i + j, hd), lax.rem(k + e, kv)), device_id_type=pl.DeviceIdType.MESH
            )
    pl.semaphore_wait(barrier, tg * hd - 1 + (kv - 1) * hd)


def plane_peer(d):
    t, i, k = place()
    _, hd, kv = sizes()
    share = 2 if hd % 2 == 0 else 1
    chips = hd // share
    core = lax.rem(i, share)
    p = lax.rem(k * chips + i // share + d + chips * kv, chips * kv)
    return lax.rem(p, chips) * share + core, p // chips


def gather_kernel(prompt, qb, info_ref, kv_ref, q_ref, wt_ref, gy_ref,
                  kvall_ref, qall_ref, o_ref, lse_ref, y_ref, do_ref,
                  wtall_ref, gyall_ref, ga_ref, vt_ref, m_ref, l_ref, acc_ref,
                  kv_sem, q_sem, w_sem, first_up, first_down, up_sem, down_sem, g_sem, f_sem, own_sem):
    t, i, k = place()
    tg, hd, n_kv = sizes()
    tok = q_ref.shape[0]
    wide = q_ref.shape[1]
    wrows = wt_ref.shape[0]
    n = tg * hd
    c = t * hd + i
    share = 2 if hd % 2 == 0 else 1
    ring = hd // share * n_kv
    greet()

    def at(p):
        return p // hd, lax.rem(p, hd)

    own = [
        pltpu.make_async_copy(kv_ref.at[:, span(i, 2 * HD)], kvall_ref.at[span(c, tok), :], own_sem.at[0]),
        pltpu.make_async_copy(q_ref.at[:, span(i, G * HD)], qall_ref.at[span(i, tok), :], own_sem.at[1]),
        pltpu.make_async_copy(wt_ref.at[:, span(i, G * HD)], wtall_ref.at[span(c, wrows), :], own_sem.at[2]),
        pltpu.make_async_copy(gy_ref, gyall_ref.at[span(i, tok), span(k, wide)], own_sem.at[3]),
    ]
    for copy in own:
        copy.start()

    def kv_copy(d, to):
        tt, ii = at(lax.rem(c + d, n))
        src = c if to else lax.rem(c - d + n, n)
        return remote(kv_ref.at[:, span(ii, 2 * HD)], kvall_ref.at[span(src, tok), :], kv_sem, d, (tt, ii, k))

    def q_copy(d, to):
        ii = lax.rem(i + d, hd)
        src = i if to else lax.rem(i - d + hd, hd)
        return remote(q_ref.at[:, span(ii, G * HD)], qall_ref.at[span(src, tok), :], q_sem, d, (t, ii, k))

    def w_copy(d, to):
        ii = lax.rem(i + d, hd)
        src = i if to else lax.rem(i - d + hd, hd)
        return remote(wt_ref.at[:, span(ii, G * HD)], wtall_ref.at[span(t * hd + src, wrows), :], w_sem, d, (t, ii, k))

    def first_hop(d, step, to):
        src = lax.rem(i - d + hd, hd)
        rows = span((t if to else t - step) * hd + src, wrows)
        block = wtall_ref.at[rows, :]
        out = wt_ref.at[:, span(i, G * HD)] if d == 0 else block
        return remote(out, block, first_up if step > 0 else first_down, d, (t + step, i, k))

    def hop(h, step, to):
        block = wtall_ref.at[span(t - step * (h if to else h + 1), wrows * hd), :]
        return remote(block, block, up_sem if step > 0 else down_sem, h, (t + step, i, k))

    def has(h, step):
        return t >= h if step > 0 else t + h < tg

    def more(step):
        return t < tg - 1 if step > 0 else t > 0

    def arrive_first():
        for step in (1, -1):
            @pl.when(has(1, step))
            def _():
                for d in range(hd):
                    first_hop(d, step, False).wait_recv()

            if tg > 2:
                @pl.when(has(1, step) & more(step))
                def _():
                    hop(1, step, True).start()

    def arrive(h):
        for step in (1, -1):
            @pl.when(has(h, step))
            def _():
                hop(h - 1, step, False).wait_recv()

            @pl.when(has(h, step) & more(step) & (h < tg - 1))
            def _():
                hop(h, step, True).start()

    part = wtall_ref.shape[0] // 4 if wrows * hd % HD else wrows * hd

    def project(u):
        cols = span(u, part)

        def tile(r, carry):
            rows = span(r, qb)
            w = wtall_ref[cols, :]
            ga_ref[rows, :] += dot(gyall_ref[rows, cols], w)
            y_ref[rows, cols] = dot(o_ref[rows, :], w, NT).astype(BF)
            return carry

        lax.fori_loop(0, o_ref.shape[0] // qb, tile, 0)

    def project_far(h):
        if wrows * hd % HD == 0:
            for step in (1, -1):
                @pl.when(has(h, step))
                def _():
                    project(t - step * h)

    def g_copy(d, to):
        ii, kk = plane_peer(d)
        si, sk = (i, k) if to else plane_peer(-d)
        return remote(gy_ref, gyall_ref.at[span(si, tok), span(sk, wide)], g_sem, d, (t, ii, kk))

    def f_copy(d, to):
        si, sk = plane_peer(-d)
        if not to:
            si = si + 1 - 2 * lax.rem(si, 2)
        block = gyall_ref.at[span(si, tok), span(sk, wide)]
        return remote(gy_ref if d == 0 else block, block, f_sem, d, (t, i + 1 - 2 * lax.rem(i, 2), k))

    for d in range(1, n):
        kv_copy(d, True).start()
    for d in range(1, hd):
        w_copy(d, True).start()
    for d in range(1, hd):
        q_copy(d, True).start()
    for step in (1, -1):
        @pl.when(more(step))
        def _():
            first_hop(0, step, True).start()
    for d in range(1, ring):
        g_copy(d, True).start()
    if share == 2:
        f_copy(0, True).start()
    for d in range(1, hd):
        w_copy(d, False).wait_recv()
        for step in (1, -1):
            @pl.when(more(step))
            def _():
                first_hop(d, step, True).start()

    ga_ref[...] = jnp.zeros_like(ga_ref)
    own[0].wait()
    own[1].wait()
    for d in range(1, n):
        kv_copy(d, False).wait_recv()
    for d in range(1, hd):
        q_copy(d, False).wait_recv()

    def turn(b, carry):
        keys = span(b, KB)
        vt_ref[:, keys] = kvall_ref[keys, HD:].T
        return carry

    lax.fori_loop(0, kvall_ref.shape[0] // KB, turn, 0)
    blocks = o_ref.shape[0] // qb
    fwd_body(prompt, qb, info_ref, qall_ref, kvall_ref, vt_ref, o_ref, lse_ref, m_ref, l_ref, acc_ref,
             arrive_first, max(blocks - 2, 0))

    for d in range(1, ring):
        g_copy(d, False).wait_recv()
        if share == 2:
            f_copy(d, True).start()
    if tg > 2:
        arrive(2)
    if share == 2:
        for d in range(ring):
            f_copy(d, False).wait_recv()
    own[2].wait()
    own[3].wait()
    if wrows * hd % HD == 0:
        project(t)

    def step_far(h, carry):
        project_far(h)
        arrive(h + 2)
        return carry

    lax.fori_loop(1, tg - 2, step_far, 0)
    for h in range(max(tg - 2, 1), tg):
        project_far(h)
    if wrows * hd % HD:
        lax.fori_loop(0, 4, lambda u, carry: (project(u), carry)[1], 0)
    do_ref[...] = ga_ref[...].astype(BF)

    if share == 2:
        for d in range(ring):
            f_copy(d, True).wait_send()
    for d in range(1, n):
        kv_copy(d, True).wait_send()
    for d in range(1, hd):
        w_copy(d, True).wait_send()
        q_copy(d, True).wait_send()
    for d in range(1, ring):
        g_copy(d, True).wait_send()
    for step in (1, -1):
        @pl.when(more(step))
        def _():
            for d in range(hd):
                first_hop(d, step, True).wait_send()

        def sent(h, carry):
            @pl.when(has(h, step) & more(step))
            def _():
                hop(h, step, True).wait_send()

            return carry

        lax.fori_loop(1, tg - 1, sent, 0)


def scatter_kernel(prompt, qb, info_ref, y_ref, q_ref, kv_ref, o_ref, lse_ref, do_ref,
                   yout_ref, dqout_ref, dkout_ref, dvout_ref,
                   pair_ref, yin_ref, dq_ref, dkv_ref, dkvin_ref, kt_ref, qs_ref, dos_ref, del_ref, p_ref, ds_ref,
                   dqt_ref, dk_ref, dv_ref, pair_sem, y_sem, dq_sem, dkv_sem, own_sem):
    t, i, k = place()
    tg, hd, n_kv = sizes()
    tok, wide = yout_ref.shape
    n = tg * hd
    c = t * hd + i
    share = 2 if hd % 2 == 0 else 1
    ring = hd // share * n_kv
    greet()
    other = i + 1 - 2 * lax.rem(i, 2)

    def pair_copy(d):
        ii, kk = plane_peer(d)
        ii = ii + 1 - 2 * lax.rem(ii, 2)
        return remote(y_ref.at[span(ii, tok), span(kk, wide)], pair_ref.at[d], pair_sem, d, (t, other, k))

    def y_copy(d):
        ii, kk = plane_peer(d)
        src = pair_ref.at[d] if share == 2 else y_ref.at[span(ii, tok), span(kk, wide)]
        return remote(src, yin_ref.at[d], y_sem, d, (t, ii, kk))

    if share == 2:
        for d in range(ring):
            pair_copy(d).start()
    else:
        for d in range(1, ring):
            y_copy(d).start()

    def turn(b, carry):
        keys = span(b, KB)
        kt_ref[:, keys] = kv_ref[keys, :HD].T
        return carry

    lax.fori_loop(0, kv_ref.shape[0] // KB, turn, 0)

    def pair_sums():
        for d in [*range(1, ring), 0]:
            pair_copy(d).wait_recv()
            ii, kk = plane_peer(d)

            def add(r, carry):
                rows = span(r, 16)
                mine = y_ref[pl.ds(pl.multiple_of(ii * tok + r * 16, 16), 16), span(kk, wide)]
                pair_ref[d, rows, :] = (pair_ref[d, rows, :].astype(jnp.float32) + mine.astype(jnp.float32)).astype(jnp.bfloat16)
                return carry

            lax.fori_loop(0, tok // 16, add, 0)
            if d:
                y_copy(d).start()

    def dkv_copy(d, to):
        p = lax.rem(c + d, n)
        src = c if to else lax.rem(c - d + n, n)
        return remote(dkv_ref.at[span(p, tok), :], dkvin_ref.at[src], dkv_sem, d, (p // hd, lax.rem(p, hd), k))

    def dq_copy(d, to):
        ii = lax.rem(i + d, hd)
        src = i if to else lax.rem(i - d + hd, hd)
        return remote(dq_ref.at[span(ii, tok), :], dqout_ref.at[:, span(src, G * HD)], dq_sem, d, (t, ii, k))

    def backward(late, between):
        bwd_body(late, between, prompt, qb, info_ref, q_ref, kv_ref, kt_ref, o_ref, lse_ref, do_ref,
                 dq_ref, dkv_ref, qs_ref, dos_ref, del_ref, p_ref, ds_ref, dqt_ref, dk_ref, dv_ref)

    def push(late):
        for d in range(1, n):
            @pl.when((lax.rem(c + d, n) * tok >= prompt) == late)
            def _():
                dkv_copy(d, True).start()

    dk_ref[...] = jnp.zeros_like(dk_ref)
    dv_ref[...] = jnp.zeros_like(dv_ref)
    dqt_ref[...] = jnp.zeros_like(dqt_ref)
    backward(False, pair_sums if share == 2 else None)
    push(False)
    backward(True, None)
    push(True)
    for d in range(1, hd):
        dq_copy(d, True).start()
    own = [
        pltpu.make_async_copy(dkv_ref.at[span(c, tok), :], dkvin_ref.at[c], own_sem.at[0]),
        pltpu.make_async_copy(dq_ref.at[span(i, tok), :], dqout_ref.at[:, span(i, G * HD)], own_sem.at[1]),
    ]
    for copy in own:
        copy.start()

    for d in range(1, ring):
        y_copy(d).wait_recv()

    def y_sum(r, carry):
        rows = span(r, 16)
        if share == 2:
            total = pair_ref[0, rows, :].astype(jnp.float32)
        else:
            total = y_ref[pl.ds(pl.multiple_of(i * tok + r * 16, 16), 16), span(k, wide)].astype(jnp.float32)
        for d in range(1, ring):
            total += yin_ref[d, rows, :].astype(jnp.float32)
        yout_ref[rows, :] = total.astype(jnp.bfloat16)
        return carry

    lax.fori_loop(0, tok // 16, y_sum, 0)
    own[0].wait()
    own[1].wait()
    for d in range(1, n):
        dkv_copy(d, False).wait_recv()

    def kv_sum(r, carry):
        rows = span(r, 32)
        for j in range(hd):
            total = dkvin_ref[j, rows, :].astype(jnp.float32)
            for u in range(1, tg):
                total += dkvin_ref[u * hd + j, rows, :].astype(jnp.float32)
            cols = slice(j * HD, (j + 1) * HD)
            dkout_ref[rows, cols] = total[:, :HD].astype(jnp.bfloat16)
            dvout_ref[rows, cols] = total[:, HD:].astype(jnp.bfloat16)
        return carry

    lax.fori_loop(0, tok // 32, kv_sum, 0)
    for d in range(1, hd):
        dq_copy(d, False).wait_recv()
        dq_copy(d, True).wait_send()
    for d in range(1, n):
        dkv_copy(d, True).wait_send()
    for d in range(1, ring):
        y_copy(d).wait_send()
    if share == 2:
        for d in range(ring):
            pair_copy(d).wait_send()


def read_info(info_ref):
    return [info_ref[i] for i in range(4)]


def fwd_body(prompt, qb, info_ref, q_ref, kv_ref, vt_ref, o_ref, lse_ref, m_ref, l_ref, acc_ref, between, after):
    info = read_info(info_ref)
    first_row = lax.axis_index("tg").astype(jnp.int32) * q_ref.shape[0]
    blocks = q_ref.shape[0] // qb

    def query_block(i, carry):
        rows = pl.ds(pl.multiple_of(i * qb, qb), qb)
        q_first = first_row + i * qb
        m_ref[...] = jnp.full_like(m_ref, NEG)
        l_ref[...] = jnp.zeros_like(l_ref)
        acc_ref[...] = jnp.zeros_like(acc_ref)
        full, last = block_range(q_first, qb, prompt)

        def key_block(masked, b, carry):
            keys = pl.ds(pl.multiple_of(b * KB, KB), KB)
            k_blk = kv_ref[keys, :HD]
            vt_blk = vt_ref[:, keys]
            vis = visible(info, q_first, qb, b * KB, prompt) if masked else None
            for h in range(G):
                s = dot(k_blk, q_ref[rows, h * HD:(h + 1) * HD], NT) * C2
                if masked:
                    s = jnp.where(vis, s, NEG)
                m_old = m_ref[h:h + 1, :]
                m_new = jnp.maximum(m_old, jnp.max(s, axis=0, keepdims=True))
                p = jnp.exp2(s - m_new)
                alpha = jnp.exp2(m_old - m_new)
                m_ref[h:h + 1, :] = m_new
                l_ref[h:h + 1, :] = l_ref[h:h + 1, :] * alpha + jnp.sum(p, axis=0, keepdims=True)
                acc_ref[h] = acc_ref[h] * alpha + dot(vt_blk, p.astype(jnp.bfloat16))
            return carry

        lax.fori_loop(0, full, functools.partial(key_block, False), 0)
        lax.fori_loop(full, last, functools.partial(key_block, True), 0)
        for h in range(G):
            l = l_ref[h:h + 1, :]
            o_ref[rows, h * HD:(h + 1) * HD] = (acc_ref[h] / l).T.astype(jnp.bfloat16)
            lse_ref[i, h:h + 1, :] = m_ref[h:h + 1, :] + jnp.log2(l)
        pl.when(i == after)(between)
        return carry

    lax.fori_loop(0, blocks, query_block, 0)


def bwd_body(late, between, prompt, qb, info_ref, q_ref, kv_ref, kt_ref, o_ref, lse_ref, do_ref,
               dq_ref, dkv_ref, qs_ref, dos_ref, del_ref, p_ref, ds_ref, dqt_ref, dk_ref, dv_ref):
    info = read_info(info_ref)
    first_row = lax.axis_index("tg").astype(jnp.int32) * q_ref.shape[0]
    blocks = q_ref.shape[0] // qb

    def query_block(i, carry):
        rows = pl.ds(pl.multiple_of(i * qb, qb), qb)
        q_first = first_row + i * qb
        for h in range(G):
            cols = slice(h * HD, (h + 1) * HD)
            do = do_ref[rows, cols]
            qs_ref[h * qb:(h + 1) * qb, :] = q_ref[rows, cols]
            dos_ref[h * qb:(h + 1) * qb, :] = do
            prod = do.astype(jnp.float32) * o_ref[rows, cols].astype(jnp.float32)
            del_ref[h:h + 1, :] = jnp.sum(prod.T, axis=0, keepdims=True)
        full, last = block_range(q_first, qb, prompt)

        def key_block(masked, b, carry):
            keys = pl.ds(pl.multiple_of(b * KB, KB), KB)
            k_blk = kv_ref[keys, :HD]
            v_blk = kv_ref[keys, HD:]
            vis = visible(info, q_first, qb, b * KB, prompt) if masked else None
            for h in range(G):
                part = slice(h * qb, (h + 1) * qb)
                s = dot(k_blk, qs_ref[part, :], NT) * C2
                p = jnp.exp2(s - lse_ref[i, h:h + 1, :])
                if masked:
                    p = jnp.where(vis, p, 0.0)
                dp = dot(v_blk, dos_ref[part, :], NT)
                p_ref[h] = p.astype(jnp.bfloat16)
                ds_ref[h] = (p * (dp - del_ref[h:h + 1, :])).astype(jnp.bfloat16)
            dv = jnp.zeros((KB, HD), jnp.float32)
            dk = jnp.zeros((KB, HD), jnp.float32)
            for h in range(G):
                part = slice(h * qb, (h + 1) * qb)
                dv += dot(p_ref[h], dos_ref[part, :])
                dk += dot(ds_ref[h], qs_ref[part, :])
                dqt_ref[i, h] += dot(kt_ref[:, keys], ds_ref[h])
            dv_ref[keys, :] += dv
            dk_ref[keys, :] += dk
            return carry

        if late:
            lax.fori_loop(jnp.maximum(full, prompt // KB), last, functools.partial(key_block, True), 0)
            for h in range(G):
                dq_ref[rows, h * HD:(h + 1) * HD] = (dqt_ref[i, h] * SCALE).T.astype(jnp.bfloat16)
        else:
            lax.fori_loop(0, full, functools.partial(key_block, False), 0)
            lax.fori_loop(full, jnp.minimum(last, prompt // KB), functools.partial(key_block, True), 0)
        if between is not None:
            pl.when(i == 0)(between)
        return carry

    lax.fori_loop(0, blocks, query_block, 0)
    half = slice(prompt, None) if late else slice(0, prompt)
    dkv_ref[half, :HD] = (dk_ref[half, :] * SCALE).astype(jnp.bfloat16)
    dkv_ref[half, HD:] = dv_ref[half, :].astype(jnp.bfloat16)


VM = pl.BlockSpec(memory_space=pltpu.VMEM)
SM = pl.BlockSpec(memory_space=pltpu.SMEM)
ANY = pl.BlockSpec(memory_space=pl.ANY)
BF = jnp.bfloat16
F32 = jnp.float32


def dma(count):
    return pltpu.SemaphoreType.DMA((2, count))


def gather_and_forward(info, kv, q, wt, gy, prompt, qb):
    tg, hd, n_kv = sizes()
    tok, n = q.shape[0], tg * hd
    rows, keys = tok * hd, tok * n
    work = G * rows * keys
    shape = jax.ShapeDtypeStruct
    return pl.pallas_call(
        functools.partial(gather_kernel, prompt, qb),
        out_shape=(
            shape((keys, 2 * HD), BF),
            shape((rows, G * HD), BF),
            shape((rows, G * HD), BF),
            shape((rows // qb, 8, qb), F32),
            shape((rows, gy.shape[1] * n_kv), BF),
            shape((rows, G * HD), BF),
        ),
        in_specs=[SM, ANY, ANY, ANY, ANY],
        out_specs=(VM,) * 6,
        scratch_shapes=[
            pltpu.VMEM((wt.shape[0] * n, G * HD), BF),
            pltpu.VMEM((rows, gy.shape[1] * n_kv), BF),
            pltpu.VMEM((rows, G * HD), F32),
            pltpu.VMEM((HD, keys), BF),
            pltpu.VMEM((8, qb), F32),
            pltpu.VMEM((8, qb), F32),
            pltpu.VMEM((G, HD, qb), F32),
            dma(n), dma(hd), dma(hd), dma(hd), dma(hd), dma(tg), dma(tg), dma(hd * n_kv), dma(hd * n_kv),
            pltpu.SemaphoreType.DMA((4,)),
        ],
        compiler_params=pltpu.CompilerParams(vmem_limit_bytes=56 << 20, collective_id=0, has_side_effects=True),
        cost_estimate=pl.CostEstimate(flops=work * HD * 4, bytes_accessed=32 << 20, transcendentals=work),
        name="gather_and_forward",
    )(info, kv, q, wt, gy)


def backward_and_scatter(info, y, q, kv, o, lse, do, tok, wide, prompt, qb):
    tg, hd, n_kv = sizes()
    n = tg * hd
    rows, keys = tok * hd, tok * n
    share = 2 if hd % 2 == 0 else 1
    ring = hd // share * n_kv
    work = G * rows * keys
    shape = jax.ShapeDtypeStruct
    return pl.pallas_call(
        functools.partial(scatter_kernel, prompt, qb),
        out_shape=(
            shape((tok, wide), BF),
            shape((tok, hd * G * HD), BF),
            shape((tok, hd * HD), BF),
            shape((tok, hd * HD), BF),
        ),
        in_specs=[SM] + [VM] * 6,
        out_specs=(VM,) * 4,
        scratch_shapes=[
            pltpu.VMEM((ring if share == 2 else 1, tok, wide), BF),
            pltpu.VMEM((ring, tok, wide), BF),
            pltpu.VMEM((rows, G * HD), BF),
            pltpu.VMEM((keys, 2 * HD), BF),
            pltpu.VMEM((n, tok, 2 * HD), BF),
            pltpu.VMEM((HD, keys), BF),
            pltpu.VMEM((G * qb, HD), BF),
            pltpu.VMEM((G * qb, HD), BF),
            pltpu.VMEM((8, qb), F32),
            pltpu.VMEM((G, KB, qb), BF),
            pltpu.VMEM((G, KB, qb), BF),
            pltpu.VMEM((rows // qb, G, HD, qb), F32),
            pltpu.VMEM((keys, HD), F32),
            pltpu.VMEM((keys, HD), F32),
            dma(ring), dma(ring), dma(hd), dma(n),
            pltpu.SemaphoreType.DMA((2,)),
        ],
        compiler_params=pltpu.CompilerParams(vmem_limit_bytes=56 << 20, collective_id=1, has_side_effects=True),
        cost_estimate=pl.CostEstimate(flops=work * HD * 10, bytes_accessed=32 << 20, transcendentals=work),
        name="backward_and_scatter",
    )(info, y, q, kv, o, lse, do)


def local(queries, keys, values, w_out, grad_y, resp_blocks):
    heads = lax.axis_size("hd")
    tok = queries.shape[0]
    rows = tok * heads
    prompt = rows * lax.axis_size("tg") // 2
    qb = 256 if rows % 256 == 0 else rows
    ends = prompt + jnp.cumsum(resp_blocks[: NRESP - 1]).astype(jnp.int32) * BLK
    info = jnp.concatenate([jnp.zeros((1,), jnp.int32), ends])
    kv = jnp.concatenate([keys.reshape(tok, heads, HD), values.reshape(tok, heads, HD)], axis=2)
    kv = kv.reshape(tok, heads * 2 * HD)
    kv_all, q, attn, lse, y, grad_attn = gather_and_forward(info, kv, queries, w_out.T, grad_y, prompt, qb)
    return backward_and_scatter(info, y, q, kv_all, attn, lse, grad_attn, tok, grad_y.shape[1], prompt, qb)


def solution(mesh):
    ctx, n_kv = mesh.devices.shape
    heads = KVH // n_kv
    split = Mesh(mesh.devices.reshape(ctx // heads, heads, n_kv), ("tg", "hd", "kv"))
    tok = ("tg", "hd")
    tiled = P(tok, "kv")
    return jax.shard_map(
        local,
        mesh=split,
        in_specs=(tiled, tiled, tiled, P("kv", tok), tiled, P()),
        out_specs=(tiled,) * 4,
        check_vma=False,
    )
```

```python
import functools
import math

import jax
import jax.numpy as jnp
from jax import lax
from jax.experimental import pallas as pl
from jax.experimental.pallas import tpu as pltpu
from jax.sharding import Mesh, PartitionSpec as P

H = 40
KVH = 8
HD = 128
BLK = 128
NRESP = 4
G = H // KVH
KB = 256
NEG = -1e30
SCALE = 1.0 / math.sqrt(HD)
C2 = SCALE * math.log2(math.e)
NT = (((1,), (1,)), ((), ()))
NN = (((1,), (0,)), ((), ()))


def dot(a, b, dims=NN):
    return lax.dot_general(a, b, dims, preferred_element_type=jnp.float32)


def seg_start(info, pos, prompt):
    start = jnp.where(pos >= info[1], info[1], prompt)
    start = jnp.where(pos >= info[2], info[2], start)
    return jnp.where(pos >= info[3], info[3], start)


def block_range(q_first, q_rows, prompt):
    full = jnp.minimum(prompt, q_first + 1) // KB
    return full, (q_first + q_rows - 1) // KB + 1


def visible(info, q_first, q_rows, k_first, prompt):
    q_pos = q_first + lax.broadcasted_iota(jnp.int32, (1, q_rows), 1)
    start = seg_start(info, q_pos, prompt)
    k_pos = k_first + lax.broadcasted_iota(jnp.int32, (KB, q_rows), 0)
    return (k_pos <= q_pos) & ((k_pos < prompt) | (k_pos >= start))


def place():
    me = lax.axis_index("tg"), lax.axis_index("hd"), lax.axis_index("kv")
    return [x.astype(jnp.int32) for x in me]


def sizes():
    return lax.axis_size("tg"), lax.axis_size("hd"), lax.axis_size("kv")


def span(index, size):
    return pl.ds(pl.multiple_of(index * size, size), size)


def remote(src, dst, sems, slot, target):
    return pltpu.make_async_remote_copy(
        src_ref=src,
        dst_ref=dst,
        send_sem=sems.at[0, slot],
        recv_sem=sems.at[1, slot],
        device_id=target,
        device_id_type=pl.DeviceIdType.MESH,
    )


def greet():
    t, i, k = place()
    tg, hd, kv = sizes()
    barrier = pltpu.get_barrier_semaphore()
    c = t * hd + i
    for d in range(1, tg * hd):
        p = lax.rem(c + d, tg * hd)
        pl.semaphore_signal(barrier, inc=1, device_id=(p // hd, lax.rem(p, hd), k), device_id_type=pl.DeviceIdType.MESH)
    for e in range(1, kv):
        for j in range(hd):
            pl.semaphore_signal(
                barrier, inc=1, device_id=(t, lax.rem(i + j, hd), lax.rem(k + e, kv)), device_id_type=pl.DeviceIdType.MESH
            )
    pl.semaphore_wait(barrier, tg * hd - 1 + (kv - 1) * hd)


def plane_peer(d):
    t, i, k = place()
    _, hd, kv = sizes()
    share = 2 if hd % 2 == 0 else 1
    chips = hd // share
    core = lax.rem(i, share)
    p = lax.rem(k * chips + i // share + d + chips * kv, chips * kv)
    return lax.rem(p, chips) * share + core, p // chips


def gather_kernel(prompt, qb, info_ref, kv_ref, q_ref, wt_ref, gy_ref,
                  kvall_ref, qall_ref, o_ref, lse_ref, y_ref, do_ref,
                  wtall_ref, gyall_ref, ga_ref, vt_ref, m_ref, l_ref, acc_ref,
                  kv_sem, q_sem, w_sem, first_up, first_down, up_sem, down_sem, g_sem, f_sem, own_sem):
    t, i, k = place()
    tg, hd, n_kv = sizes()
    tok = q_ref.shape[0]
    wide = q_ref.shape[1]
    wrows = wt_ref.shape[0]
    n = tg * hd
    c = t * hd + i
    share = 2 if hd % 2 == 0 else 1
    ring = hd // share * n_kv
    greet()

    def at(p):
        return p // hd, lax.rem(p, hd)

    own = [
        pltpu.make_async_copy(kv_ref.at[:, span(i, 2 * HD)], kvall_ref.at[span(c, tok), :], own_sem.at[0]),
        pltpu.make_async_copy(q_ref.at[:, span(i, G * HD)], qall_ref.at[span(i, tok), :], own_sem.at[1]),
        pltpu.make_async_copy(wt_ref.at[:, span(i, G * HD)], wtall_ref.at[span(c, wrows), :], own_sem.at[2]),
        pltpu.make_async_copy(gy_ref, gyall_ref.at[span(i, tok), span(k, wide)], own_sem.at[3]),
    ]
    for copy in own:
        copy.start()

    def kv_copy(d, to):
        tt, ii = at(lax.rem(c + d, n))
        src = c if to else lax.rem(c - d + n, n)
        return remote(kv_ref.at[:, span(ii, 2 * HD)], kvall_ref.at[span(src, tok), :], kv_sem, d, (tt, ii, k))

    def q_copy(d, to):
        ii = lax.rem(i + d, hd)
        src = i if to else lax.rem(i - d + hd, hd)
        return remote(q_ref.at[:, span(ii, G * HD)], qall_ref.at[span(src, tok), :], q_sem, d, (t, ii, k))

    def w_copy(d, to):
        ii = lax.rem(i + d, hd)
        src = i if to else lax.rem(i - d + hd, hd)
        return remote(wt_ref.at[:, span(ii, G * HD)], wtall_ref.at[span(t * hd + src, wrows), :], w_sem, d, (t, ii, k))

    def first_hop(d, step, to):
        src = lax.rem(i - d + hd, hd)
        rows = span((t if to else t - step) * hd + src, wrows)
        block = wtall_ref.at[rows, :]
        out = wt_ref.at[:, span(i, G * HD)] if d == 0 else block
        return remote(out, block, first_up if step > 0 else first_down, d, (t + step, i, k))

    def hop(h, step, to):
        block = wtall_ref.at[span(t - step * (h if to else h + 1), wrows * hd), :]
        return remote(block, block, up_sem if step > 0 else down_sem, h, (t + step, i, k))

    def has(h, step):
        return t >= h if step > 0 else t + h < tg

    def more(step):
        return t < tg - 1 if step > 0 else t > 0

    def arrive_first():
        for step in (1, -1):
            @pl.when(has(1, step))
            def _():
                for d in range(hd):
                    first_hop(d, step, False).wait_recv()

            if tg > 2:
                @pl.when(has(1, step) & more(step))
                def _():
                    hop(1, step, True).start()

    def arrive(h):
        for step in (1, -1):
            @pl.when(has(h, step))
            def _():
                hop(h - 1, step, False).wait_recv()

            @pl.when(has(h, step) & more(step) & (h < tg - 1))
            def _():
                hop(h, step, True).start()

    part = wtall_ref.shape[0] // 4 if wrows * hd % HD else wrows * hd

    def project(u):
        cols = span(u, part)

        def tile(r, carry):
            rows = span(r, qb)
            w = wtall_ref[cols, :]
            ga_ref[rows, :] += dot(gyall_ref[rows, cols], w)
            y_ref[rows, cols] = dot(o_ref[rows, :], w, NT).astype(BF)
            return carry

        lax.fori_loop(0, o_ref.shape[0] // qb, tile, 0)

    def project_far(h):
        if wrows * hd % HD == 0:
            for step in (1, -1):
                @pl.when(has(h, step))
                def _():
                    project(t - step * h)

    def g_copy(d, to):
        ii, kk = plane_peer(d)
        si, sk = (i, k) if to else plane_peer(-d)
        return remote(gy_ref, gyall_ref.at[span(si, tok), span(sk, wide)], g_sem, d, (t, ii, kk))

    def f_copy(d, to):
        si, sk = plane_peer(-d)
        if not to:
            si = si + 1 - 2 * lax.rem(si, 2)
        block = gyall_ref.at[span(si, tok), span(sk, wide)]
        return remote(gy_ref if d == 0 else block, block, f_sem, d, (t, i + 1 - 2 * lax.rem(i, 2), k))

    for d in range(1, n):
        kv_copy(d, True).start()
    for d in range(1, hd):
        w_copy(d, True).start()
    for d in range(1, hd):
        q_copy(d, True).start()
    for step in (1, -1):
        @pl.when(more(step))
        def _():
            first_hop(0, step, True).start()
    for d in range(1, ring):
        g_copy(d, True).start()
    if share == 2:
        f_copy(0, True).start()
    for d in range(1, hd):
        w_copy(d, False).wait_recv()
        for step in (1, -1):
            @pl.when(more(step))
            def _():
                first_hop(d, step, True).start()

    ga_ref[...] = jnp.zeros_like(ga_ref)
    own[0].wait()
    own[1].wait()
    for d in range(1, n):
        kv_copy(d, False).wait_recv()
    for d in range(1, hd):
        q_copy(d, False).wait_recv()

    def turn(b, carry):
        keys = span(b, KB)
        vt_ref[:, keys] = kvall_ref[keys, HD:].T
        return carry

    lax.fori_loop(0, kvall_ref.shape[0] // KB, turn, 0)
    fwd_body(prompt, qb, info_ref, qall_ref, kvall_ref, vt_ref, o_ref, lse_ref, m_ref, l_ref, acc_ref,
             arrive_first, 0)

    for d in range(1, ring):
        g_copy(d, False).wait_recv()
        if share == 2:
            f_copy(d, True).start()
    if share == 2:
        for d in range(ring):
            f_copy(d, False).wait_recv()
    own[2].wait()
    own[3].wait()
    if wrows * hd % HD == 0:
        project(t)

    def step_far(h, carry):
        arrive(h + 1)
        project_far(h)
        return carry

    lax.fori_loop(1, tg - 1, step_far, 0)
    project_far(tg - 1)
    if wrows * hd % HD:
        lax.fori_loop(0, 4, lambda u, carry: (project(u), carry)[1], 0)
    do_ref[...] = ga_ref[...].astype(BF)

    if share == 2:
        for d in range(ring):
            f_copy(d, True).wait_send()
    for d in range(1, n):
        kv_copy(d, True).wait_send()
    for d in range(1, hd):
        w_copy(d, True).wait_send()
        q_copy(d, True).wait_send()
    for d in range(1, ring):
        g_copy(d, True).wait_send()
    for step in (1, -1):
        @pl.when(more(step))
        def _():
            for d in range(hd):
                first_hop(d, step, True).wait_send()

        def sent(h, carry):
            @pl.when(has(h, step) & more(step))
            def _():
                hop(h, step, True).wait_send()

            return carry

        lax.fori_loop(1, tg - 1, sent, 0)


def scatter_kernel(prompt, qb, info_ref, y_ref, q_ref, kv_ref, o_ref, lse_ref, do_ref,
                   yout_ref, dqout_ref, dkout_ref, dvout_ref,
                   pair_ref, yin_ref, dq_ref, dkv_ref, dkvin_ref, kt_ref, qs_ref, dos_ref, del_ref, p_ref, ds_ref,
                   dqt_ref, dk_ref, dv_ref, pair_sem, y_sem, dq_sem, dkv_sem, own_sem):
    t, i, k = place()
    tg, hd, n_kv = sizes()
    tok, wide = yout_ref.shape
    n = tg * hd
    c = t * hd + i
    share = 2 if hd % 2 == 0 else 1
    ring = hd // share * n_kv
    greet()
    other = i + 1 - 2 * lax.rem(i, 2)

    def pair_copy(d):
        ii, kk = plane_peer(d)
        ii = ii + 1 - 2 * lax.rem(ii, 2)
        return remote(y_ref.at[span(ii, tok), span(kk, wide)], pair_ref.at[d], pair_sem, d, (t, other, k))

    def y_copy(d):
        ii, kk = plane_peer(d)
        src = pair_ref.at[d] if share == 2 else y_ref.at[span(ii, tok), span(kk, wide)]
        return remote(src, yin_ref.at[d], y_sem, d, (t, ii, kk))

    if share == 2:
        for d in range(ring):
            pair_copy(d).start()
    else:
        for d in range(1, ring):
            y_copy(d).start()

    def turn(b, carry):
        keys = span(b, KB)
        kt_ref[:, keys] = kv_ref[keys, :HD].T
        return carry

    lax.fori_loop(0, kv_ref.shape[0] // KB, turn, 0)

    if share == 2:
        for d in [*range(1, ring), 0]:
            pair_copy(d).wait_recv()
            ii, kk = plane_peer(d)

            def add(r, carry):
                rows = span(r, 16)
                mine = y_ref[pl.ds(pl.multiple_of(ii * tok + r * 16, 16), 16), span(kk, wide)]
                pair_ref[d, rows, :] = (pair_ref[d, rows, :].astype(jnp.float32) + mine.astype(jnp.float32)).astype(jnp.bfloat16)
                return carry

            lax.fori_loop(0, tok // 16, add, 0)
            if d:
                y_copy(d).start()

    bwd_body(prompt, qb, info_ref, q_ref, kv_ref, kt_ref, o_ref, lse_ref, do_ref,
             dq_ref, dkv_ref, qs_ref, dos_ref, del_ref, p_ref, ds_ref, dqt_ref, dk_ref, dv_ref)

    def dkv_copy(d, to):
        p = lax.rem(c + d, n)
        src = c if to else lax.rem(c - d + n, n)
        return remote(dkv_ref.at[span(p, tok), :], dkvin_ref.at[src], dkv_sem, d, (p // hd, lax.rem(p, hd), k))

    def dq_copy(d, to):
        ii = lax.rem(i + d, hd)
        src = i if to else lax.rem(i - d + hd, hd)
        return remote(dq_ref.at[span(ii, tok), :], dqout_ref.at[:, span(src, G * HD)], dq_sem, d, (t, ii, k))

    for d in range(1, n):
        dkv_copy(d, True).start()
    for d in range(1, hd):
        dq_copy(d, True).start()
    own = [
        pltpu.make_async_copy(dkv_ref.at[span(c, tok), :], dkvin_ref.at[c], own_sem.at[0]),
        pltpu.make_async_copy(dq_ref.at[span(i, tok), :], dqout_ref.at[:, span(i, G * HD)], own_sem.at[1]),
    ]
    for copy in own:
        copy.start()

    for d in range(1, ring):
        y_copy(d).wait_recv()

    def y_sum(r, carry):
        rows = span(r, 16)
        if share == 2:
            total = pair_ref[0, rows, :].astype(jnp.float32)
        else:
            total = y_ref[pl.ds(pl.multiple_of(i * tok + r * 16, 16), 16), span(k, wide)].astype(jnp.float32)
        for d in range(1, ring):
            total += yin_ref[d, rows, :].astype(jnp.float32)
        yout_ref[rows, :] = total.astype(jnp.bfloat16)
        return carry

    lax.fori_loop(0, tok // 16, y_sum, 0)
    own[0].wait()
    own[1].wait()
    for d in range(1, n):
        dkv_copy(d, False).wait_recv()

    def kv_sum(r, carry):
        rows = span(r, 32)
        for j in range(hd):
            total = dkvin_ref[j, rows, :].astype(jnp.float32)
            for u in range(1, tg):
                total += dkvin_ref[u * hd + j, rows, :].astype(jnp.float32)
            cols = slice(j * HD, (j + 1) * HD)
            dkout_ref[rows, cols] = total[:, :HD].astype(jnp.bfloat16)
            dvout_ref[rows, cols] = total[:, HD:].astype(jnp.bfloat16)
        return carry

    lax.fori_loop(0, tok // 32, kv_sum, 0)
    for d in range(1, hd):
        dq_copy(d, False).wait_recv()
        dq_copy(d, True).wait_send()
    for d in range(1, n):
        dkv_copy(d, True).wait_send()
    for d in range(1, ring):
        y_copy(d).wait_send()
    if share == 2:
        for d in range(ring):
            pair_copy(d).wait_send()


def read_info(info_ref):
    return [info_ref[i] for i in range(4)]


def fwd_body(prompt, qb, info_ref, q_ref, kv_ref, vt_ref, o_ref, lse_ref, m_ref, l_ref, acc_ref, between, after):
    info = read_info(info_ref)
    first_row = lax.axis_index("tg").astype(jnp.int32) * q_ref.shape[0]
    blocks = q_ref.shape[0] // qb

    def query_block(i, carry):
        rows = pl.ds(pl.multiple_of(i * qb, qb), qb)
        q_first = first_row + i * qb
        m_ref[...] = jnp.full_like(m_ref, NEG)
        l_ref[...] = jnp.zeros_like(l_ref)
        acc_ref[...] = jnp.zeros_like(acc_ref)
        full, last = block_range(q_first, qb, prompt)

        def key_block(masked, b, carry):
            keys = pl.ds(pl.multiple_of(b * KB, KB), KB)
            k_blk = kv_ref[keys, :HD]
            vt_blk = vt_ref[:, keys]
            vis = visible(info, q_first, qb, b * KB, prompt) if masked else None
            for h in range(G):
                s = dot(k_blk, q_ref[rows, h * HD:(h + 1) * HD], NT) * C2
                if masked:
                    s = jnp.where(vis, s, NEG)
                m_old = m_ref[h:h + 1, :]
                m_new = jnp.maximum(m_old, jnp.max(s, axis=0, keepdims=True))
                p = jnp.exp2(s - m_new)
                alpha = jnp.exp2(m_old - m_new)
                m_ref[h:h + 1, :] = m_new
                l_ref[h:h + 1, :] = l_ref[h:h + 1, :] * alpha + jnp.sum(p, axis=0, keepdims=True)
                acc_ref[h] = acc_ref[h] * alpha + dot(vt_blk, p.astype(jnp.bfloat16))
            return carry

        lax.fori_loop(0, full, functools.partial(key_block, False), 0)
        lax.fori_loop(full, last, functools.partial(key_block, True), 0)
        for h in range(G):
            l = l_ref[h:h + 1, :]
            o_ref[rows, h * HD:(h + 1) * HD] = (acc_ref[h] / l).T.astype(jnp.bfloat16)
            lse_ref[i, h:h + 1, :] = m_ref[h:h + 1, :] + jnp.log2(l)
        pl.when(i == after)(between)
        return carry

    lax.fori_loop(0, blocks, query_block, 0)


def bwd_body(prompt, qb, info_ref, q_ref, kv_ref, kt_ref, o_ref, lse_ref, do_ref,
               dq_ref, dkv_ref, qs_ref, dos_ref, del_ref, p_ref, ds_ref, dqt_ref, dk_ref, dv_ref):
    info = read_info(info_ref)
    first_row = lax.axis_index("tg").astype(jnp.int32) * q_ref.shape[0]
    blocks = q_ref.shape[0] // qb
    dk_ref[...] = jnp.zeros_like(dk_ref)
    dv_ref[...] = jnp.zeros_like(dv_ref)

    def query_block(i, carry):
        rows = pl.ds(pl.multiple_of(i * qb, qb), qb)
        q_first = first_row + i * qb
        for h in range(G):
            cols = slice(h * HD, (h + 1) * HD)
            do = do_ref[rows, cols]
            qs_ref[h * qb:(h + 1) * qb, :] = q_ref[rows, cols]
            dos_ref[h * qb:(h + 1) * qb, :] = do
            prod = do.astype(jnp.float32) * o_ref[rows, cols].astype(jnp.float32)
            del_ref[h:h + 1, :] = jnp.sum(prod.T, axis=0, keepdims=True)
        dqt_ref[...] = jnp.zeros_like(dqt_ref)
        full, last = block_range(q_first, qb, prompt)

        def key_block(masked, b, carry):
            keys = pl.ds(pl.multiple_of(b * KB, KB), KB)
            k_blk = kv_ref[keys, :HD]
            v_blk = kv_ref[keys, HD:]
            vis = visible(info, q_first, qb, b * KB, prompt) if masked else None
            for h in range(G):
                part = slice(h * qb, (h + 1) * qb)
                s = dot(k_blk, qs_ref[part, :], NT) * C2
                p = jnp.exp2(s - lse_ref[i, h:h + 1, :])
                if masked:
                    p = jnp.where(vis, p, 0.0)
                dp = dot(v_blk, dos_ref[part, :], NT)
                p_ref[h] = p.astype(jnp.bfloat16)
                ds_ref[h] = (p * (dp - del_ref[h:h + 1, :])).astype(jnp.bfloat16)
            dv = jnp.zeros((KB, HD), jnp.float32)
            dk = jnp.zeros((KB, HD), jnp.float32)
            for h in range(G):
                part = slice(h * qb, (h + 1) * qb)
                dv += dot(p_ref[h], dos_ref[part, :])
                dk += dot(ds_ref[h], qs_ref[part, :])
                dqt_ref[h] += dot(kt_ref[:, keys], ds_ref[h])
            dv_ref[keys, :] += dv
            dk_ref[keys, :] += dk
            return carry

        lax.fori_loop(0, full, functools.partial(key_block, False), 0)
        lax.fori_loop(full, last, functools.partial(key_block, True), 0)
        for h in range(G):
            dq_ref[rows, h * HD:(h + 1) * HD] = (dqt_ref[h] * SCALE).T.astype(jnp.bfloat16)
        return carry

    lax.fori_loop(0, blocks, query_block, 0)
    dkv_ref[:, :HD] = (dk_ref[...] * SCALE).astype(jnp.bfloat16)
    dkv_ref[:, HD:] = dv_ref[...].astype(jnp.bfloat16)


VM = pl.BlockSpec(memory_space=pltpu.VMEM)
SM = pl.BlockSpec(memory_space=pltpu.SMEM)
ANY = pl.BlockSpec(memory_space=pl.ANY)
BF = jnp.bfloat16
F32 = jnp.float32


def dma(count):
    return pltpu.SemaphoreType.DMA((2, count))


def gather_and_forward(info, kv, q, wt, gy, prompt, qb):
    tg, hd, n_kv = sizes()
    tok, n = q.shape[0], tg * hd
    rows, keys = tok * hd, tok * n
    work = G * rows * keys
    shape = jax.ShapeDtypeStruct
    return pl.pallas_call(
        functools.partial(gather_kernel, prompt, qb),
        out_shape=(
            shape((keys, 2 * HD), BF),
            shape((rows, G * HD), BF),
            shape((rows, G * HD), BF),
            shape((rows // qb, 8, qb), F32),
            shape((rows, gy.shape[1] * n_kv), BF),
            shape((rows, G * HD), BF),
        ),
        in_specs=[SM, ANY, ANY, ANY, ANY],
        out_specs=(VM,) * 6,
        scratch_shapes=[
            pltpu.VMEM((wt.shape[0] * n, G * HD), BF),
            pltpu.VMEM((rows, gy.shape[1] * n_kv), BF),
            pltpu.VMEM((rows, G * HD), F32),
            pltpu.VMEM((HD, keys), BF),
            pltpu.VMEM((8, qb), F32),
            pltpu.VMEM((8, qb), F32),
            pltpu.VMEM((G, HD, qb), F32),
            dma(n), dma(hd), dma(hd), dma(hd), dma(hd), dma(tg), dma(tg), dma(hd * n_kv), dma(hd * n_kv),
            pltpu.SemaphoreType.DMA((4,)),
        ],
        compiler_params=pltpu.CompilerParams(vmem_limit_bytes=56 << 20, collective_id=0, has_side_effects=True),
        cost_estimate=pl.CostEstimate(flops=work * HD * 4, bytes_accessed=32 << 20, transcendentals=work),
        name="gather_and_forward",
    )(info, kv, q, wt, gy)


def backward_and_scatter(info, y, q, kv, o, lse, do, tok, wide, prompt, qb):
    tg, hd, n_kv = sizes()
    n = tg * hd
    rows, keys = tok * hd, tok * n
    share = 2 if hd % 2 == 0 else 1
    ring = hd // share * n_kv
    work = G * rows * keys
    shape = jax.ShapeDtypeStruct
    return pl.pallas_call(
        functools.partial(scatter_kernel, prompt, qb),
        out_shape=(
            shape((tok, wide), BF),
            shape((tok, hd * G * HD), BF),
            shape((tok, hd * HD), BF),
            shape((tok, hd * HD), BF),
        ),
        in_specs=[SM] + [VM] * 6,
        out_specs=(VM,) * 4,
        scratch_shapes=[
            pltpu.VMEM((ring if share == 2 else 1, tok, wide), BF),
            pltpu.VMEM((ring, tok, wide), BF),
            pltpu.VMEM((rows, G * HD), BF),
            pltpu.VMEM((keys, 2 * HD), BF),
            pltpu.VMEM((n, tok, 2 * HD), BF),
            pltpu.VMEM((HD, keys), BF),
            pltpu.VMEM((G * qb, HD), BF),
            pltpu.VMEM((G * qb, HD), BF),
            pltpu.VMEM((8, qb), F32),
            pltpu.VMEM((G, KB, qb), BF),
            pltpu.VMEM((G, KB, qb), BF),
            pltpu.VMEM((G, HD, qb), F32),
            pltpu.VMEM((keys, HD), F32),
            pltpu.VMEM((keys, HD), F32),
            dma(ring), dma(ring), dma(hd), dma(n),
            pltpu.SemaphoreType.DMA((2,)),
        ],
        compiler_params=pltpu.CompilerParams(vmem_limit_bytes=56 << 20, collective_id=1, has_side_effects=True),
        cost_estimate=pl.CostEstimate(flops=work * HD * 10, bytes_accessed=32 << 20, transcendentals=work),
        name="backward_and_scatter",
    )(info, y, q, kv, o, lse, do)


def local(queries, keys, values, w_out, grad_y, resp_blocks):
    heads = lax.axis_size("hd")
    tok = queries.shape[0]
    rows = tok * heads
    prompt = rows * lax.axis_size("tg") // 2
    qb = 256 if rows % 256 == 0 else rows
    ends = prompt + jnp.cumsum(resp_blocks[: NRESP - 1]).astype(jnp.int32) * BLK
    info = jnp.concatenate([jnp.zeros((1,), jnp.int32), ends])
    kv = jnp.concatenate([keys.reshape(tok, heads, HD), values.reshape(tok, heads, HD)], axis=2)
    kv = kv.reshape(tok, heads * 2 * HD)
    kv_all, q, attn, lse, y, grad_attn = gather_and_forward(info, kv, queries, w_out.T, grad_y, prompt, qb)
    return backward_and_scatter(info, y, q, kv_all, attn, lse, grad_attn, tok, grad_y.shape[1], prompt, qb)


def solution(mesh):
    ctx, n_kv = mesh.devices.shape
    heads = KVH // n_kv
    split = Mesh(mesh.devices.reshape(ctx // heads, heads, n_kv), ("tg", "hd", "kv"))
    tok = ("tg", "hd")
    tiled = P(tok, "kv")
    return jax.shard_map(
        local,
        mesh=split,
        in_specs=(tiled, tiled, tiled, P("kv", tok), tiled, P()),
        out_specs=(tiled,) * 4,
        check_vma=False,
    )
```
